512 devices in a mesh: freq: 8 (over y, core), fibre: 64 (over z, x).
Axes of the slice: x: 4, y: 4, z: 16, core: 2. Of those that a mesh axis runs over, the one named last changes fastest.
Arguments:
- spectra: bfloat16 [16, 2, 512, 32768], P('freq', None, None, 'fibre')
- pairs: int32 [256, 4], P('fibre'), may hold values from 0 to 255, as said below
- refs: int32 [2], replicated, may hold values from 0 to 255
Outputs:
- pair_grams: bfloat16 [16, 256, 4, 2, 128, 128], P('freq', 'fibre')
- ref_grams: bfloat16 [16, 256, 2, 2, 128, 128], P('freq', 'fibre')
The draws below stay inside these ranges and needn't reach their ends.
Inputs may be any that keep to these rules, and one draw needn't show every extreme that they name: `pairs`: each row lists 4 different blocks other than its own, none more than 4 blocks away from it; the first and the last block are partners of some row.
All inputs are finite; a program needn't handle non-finite values.
Results may differ from the reference program's by a relative error of at most 0.0057.
Values may be sent and summed in bfloat16 or wider, within the bound.
A program may use at most 64 MiB of HBM per device.

```python
import jax
import jax.numpy as jnp
from jax import lax

BLK = 128
NP = 4
REACH = 4
SEGS = 512
BLOCKS = 256
CHANNELS = 32768
FREQS = 16


def draw_spectra(key, part):
    key = jax.random.fold_in(key, 11)
    first, second = jax.random.split(key, 2)
    level = jnp.exp(jax.random.uniform(first, (FREQS, 1, 1, CHANNELS), jnp.float32, -1.2, 1.2))
    values = jax.random.normal(second, (FREQS, 2, SEGS, CHANNELS), jnp.float32) * level
    return values.astype(jnp.bfloat16)


def draw_pairs(key, part):
    key = jax.random.fold_in(key, 23)
    offsets = jnp.concatenate([jnp.arange(-REACH, 0), jnp.arange(1, REACH + 1)]).astype(jnp.int32)
    blocks = jnp.arange(BLOCKS, dtype=jnp.int32)[:, None]
    candidates = blocks + offsets[None, :]
    valid = (candidates >= 0) & (candidates < BLOCKS)
    scores = jax.random.randint(key, (BLOCKS, 2 * REACH), 0, 4096) * 64 + jnp.arange(2 * REACH, dtype=jnp.int32)[None, :]
    scores = scores + jnp.where((candidates == 0) | (candidates == BLOCKS - 1), 1 << 20, 0)
    scores = jnp.where(valid, scores, -1)
    chosen = jax.lax.top_k(scores, NP)[1]
    return jnp.take_along_axis(candidates, chosen, 1).astype(jnp.int32)


def setup_inputs(seed: int = 0) -> dict:
    keys = jax.random.split(jax.random.key(seed), 4)
    return {
        "spectra": draw_spectra(jax.random.fold_in(keys[3], 71), 0),
        "pairs": draw_pairs(jax.random.fold_in(keys[3], 71), 0),
        "refs": jax.random.randint(keys[2], (2,), 0, BLOCKS).astype(jnp.int32),
    }


EPS = 1e-06

def cross_all(left, right, rotated):
    real = jnp.einsum('sbi,sbj->bij', left, right)
    imag = jnp.einsum('sbi,sbj->bij', left, rotated)
    return jnp.stack([real, imag], 1) * (1.0 / jnp.sqrt(jnp.float32(SEGS)))

def reference(spectra, pairs, refs):
    power = lax.map(lambda piece: lax.optimization_barrier(jnp.sum(jnp.square(piece.astype(jnp.float32)), axis=(0, 1))) / SEGS, spectra)
    padded = jnp.pad(power, ((1, 1), (0, 0)))
    summed = padded[:-2] + padded[1:-1] + padded[2:]
    index = jnp.arange(FREQS)
    count = 3.0 - (index == 0).astype(jnp.float32) - (index == FREQS - 1).astype(jnp.float32)
    smooth = summed / count[:, None]

    def one_bin(items):
        piece, level = items
        whitened = (piece.astype(jnp.float32) / jnp.sqrt(level + EPS)[None, None, :]).astype(jnp.bfloat16)
        blocks = whitened.reshape(2, SEGS, BLOCKS, BLK)
        left = blocks.reshape(2 * SEGS, BLOCKS, BLK).astype(jnp.float32)
        rotated = jnp.concatenate([blocks[1], -blocks[0]], 0).astype(jnp.float32)
        pair_out = []
        for slot in range(NP):
            partner = pairs[:, slot]
            pair_out.append(cross_all(left, left[:, partner, :], rotated[:, partner, :]).astype(jnp.bfloat16))
        ref_out = []
        for which in range(2):
            partner = jnp.broadcast_to(refs[which], (BLOCKS,)).astype(jnp.int32)
            ref_out.append(cross_all(left, left[:, partner, :], rotated[:, partner, :]).astype(jnp.bfloat16))
        return (jnp.stack(pair_out, 1), jnp.stack(ref_out, 1))
    pair_grams, ref_grams = lax.map(one_bin, (spectra, smooth))
    return (pair_grams, ref_grams)
```

```python
import math

import jax
import jax.numpy as jnp
from jax import lax
from jax.experimental import pallas as pl
from jax.experimental.pallas import tpu as pltpu
from jax.sharding import PartitionSpec as P

BLK = 128
NP = 4
SEGS = 512
EPS = 1e-06
BINS = 2
NBLK = 4
CHAN = NBLK * BLK
PAIR = 2 * BLK
NX = 4
NZ = 16
NF = 8
NFIB = NX * NZ
SCALE = 1.0 / math.sqrt(SEGS)
MESH = pl.DeviceIdType.MESH
TO_RIGHT = ((0, 0), (1, 0), (1, 1))
TO_LEFT = ((2, 2), (3, 2), (3, 3))
SLOTS = 14
LEFT, OWN0, OWN1, RIGHT, REFS = range(5)


def kernel(
    refs_ref, spec_hbm, g_hbm,
    raw, white, lhs, halo, mine, ring, xsend, xrecv, full, stage, gsend, grecv,
    psend, precv, inv_own, inv_halo, mask_ref,
    load_sem, pow_s, pow_r, halo_s, halo_r, ring_s, ring_r, x_s, x_r, ag_s, ag_r,
    gs_s, gs_r, inv_s, inv_r, out_sem, far_sem,
):
    f32, bf = jnp.float32, jnp.bfloat16
    fq = lax.axis_index("freq")
    fb = lax.axis_index("fibre")
    x = lax.rem(fb, NX)
    z = fb // NX
    f_up, f_dn = lax.rem(fq + 1, NF), lax.rem(fq + NF - 1, NF)
    right, left = lax.rem(fb + 1, NFIB), lax.rem(fb + NFIB - 1, NFIB)
    z_up, z_dn = lax.rem(fb + NX, NFIB), lax.rem(fb + NFIB - NX, NFIB)
    peers = [z * NX + lax.rem(x + o, NX) for o in (1, 2, 3)]

    def remote(src, dst, s_sem, r_sem, f, d):
        return pltpu.make_async_remote_copy(
            src, dst, s_sem, r_sem, device_id=(f, d), device_id_type=MESH)

    loads = [
        pltpu.make_async_copy(
            spec_hbm.at[b, :, :, pl.ds(h * PAIR, PAIR)], raw.at[h, b], load_sem.at[b, h])
        for b in range(BINS) for h in range(2)
    ]
    for c in loads:
        c.start()

    barrier = pltpu.get_barrier_semaphore()
    for f in (f_up, f_dn):
        pl.semaphore_signal(barrier, inc=1, device_id=(f, fb), device_id_type=MESH)
    for d in [right, left, z_up, z_dn] + peers:
        pl.semaphore_signal(barrier, inc=1, device_id=(fq, d), device_id_type=MESH)

    block = fb * NBLK + lax.broadcasted_iota(jnp.int32, (16, CHAN), 1) // BLK
    for r in range(2):
        mask_ref[r] = jnp.where(block == refs_ref[r], 1.0, 0.0).astype(bf)

    def gather_lanes(t):
        return (t[..., :BLK] + t[..., BLK:2 * BLK]) + (t[..., 2 * BLK:3 * BLK] + t[..., 3 * BLK:])

    def gather_two(t):
        return t[..., :BLK] + t[..., BLK:]

    for b in range(BINS):
        loads[2 * b].wait()
        loads[2 * b + 1].wait()

        def pick(i, _, b=b):
            for part in range(2):
                v = [raw[h, b, part, pl.ds(i * 128, 128), :].reshape(8, 16, PAIR) for h in range(2)]
                for r in range(2):
                    m = mask_ref[r]
                    t = gather_two(v[0] * m[None, :, :PAIR]) + gather_two(v[1] * m[None, :, PAIR:])
                    mine[b * 8 + part * 4 + i, :, r * BLK:(r + 1) * BLK] = t.reshape(128, BLK)
            return 0

        lax.fori_loop(0, 4, pick, 0)

    def ring_copy(way, s, k):
        rows = pl.ds(k * 64, 64)
        src = mine.at[lax.rem(z + 8, NZ) if way == 0 else lax.rem(z + NZ - 7, NZ), rows]
        if not (isinstance(s, int) and s == 0):
            src = ring.at[way, s, rows]
        return remote(src, ring.at[way, s + 1, rows], ring_s.at[way, s, k], ring_r.at[way, s, k],
                      fq, z_up if way == 0 else z_dn)

    def halo_copy(b, side, part):
        return remote(raw.at[1 - side, b, part], halo.at[side, b, part], halo_s.at[side, b, part],
                      halo_r.at[side, b, part], fq, right if side == 0 else left)

    def inv_copy(side):
        cols = pl.ds(2 * BLK, 2 * BLK) if side == 0 else pl.ds(0, 2 * BLK)
        return remote(inv_own.at[:, :, cols], inv_halo.at[side], inv_s.at[side], inv_r.at[side],
                      fq, right if side == 0 else left)

    pl.semaphore_wait(barrier, 9)
    for k in range(2):
        for way in range(2):
            ring_copy(way, 0, k).start()

    def halo_start(b, part):
        for side in range(2):
            halo_copy(b, side, part).start()

    halo_start(0, 0)

    def reduce_step(s):
        for k in range(2):
            rows = pl.ds(k * 64, 64)
            ring_copy(0, s, k).wait_recv()
            ring[0, s + 1, rows] = ring[0, s + 1, rows] + mine[lax.rem(z + 7 - s + NZ, NZ), rows]
            if s < 7:
                ring_copy(0, s + 1, k).start()
            if s < 7:
                ring_copy(1, s, k).wait_recv()
            if s < 6:
                ring[1, s + 1, rows] = ring[1, s + 1, rows] + mine[lax.rem(z + NZ - 6 + s, NZ), rows]
                ring_copy(1, s + 1, k).start()

    for b in range(BINS):
        def add(i, acc, b=b):
            for part in range(2):
                v = [raw[h, b, part, pl.ds(i * 64, 64), :].astype(f32) for h in range(2)]
                acc = [a + jnp.sum((w * w).reshape(8, 8, PAIR), axis=0) for a, w in zip(acc, v)]
            return acc

        acc = lax.fori_loop(0, SEGS // 64, add, [jnp.zeros((8, PAIR), f32)] * 2)
        psend[b, :, :PAIR] = acc[0]
        psend[b, :, PAIR:] = acc[1]

    up = remote(psend.at[1], precv.at[0], pow_s.at[0], pow_r.at[0], f_up, fb)
    dn = remote(psend.at[0], precv.at[1], pow_s.at[1], pow_r.at[1], f_dn, fb)
    up.start()
    dn.start()
    reduce_step(0)

    def total(v):
        return jnp.sum(v, axis=0, keepdims=True) / SEGS

    p0, p1 = total(psend[0]), total(psend[1])
    up.wait()
    dn.wait()
    below = jnp.where(fq == 0, 0.0, total(precv[0]))
    above = jnp.where(fq == NF - 1, 0.0, total(precv[1]))
    c0 = jnp.where(fq == 0, 2.0, 3.0)
    c1 = jnp.where(fq == NF - 1, 2.0, 3.0)
    smooth = [(below + p0 + p1) / c0, (p0 + p1 + above) / c1]
    row = lax.broadcasted_iota(jnp.int32, (16, BLK), 0)
    for b in range(BINS):
        inv_own[b] = jnp.broadcast_to(1.0 / jnp.sqrt(smooth[b] + EPS), (8, CHAN))
    inv_copy(0).start()
    inv_copy(1).start()
    for r in range(2):
        tile = jnp.zeros((16, BLK), f32)
        for b in range(BINS):
            v = gather_lanes(inv_own[b, 0:1, :] * mask_ref[r, 0:1, :].astype(f32))
            for piece in range(3):
                part = v.astype(bf).astype(f32)
                tile = jnp.where(row == b * 3 + piece, jnp.broadcast_to(part, (16, BLK)), tile)
                v = v - part
        xsend[128:144, r * BLK:(r + 1) * BLK] = tile.astype(bf)
    reduce_step(1)
    halo_start(0, 1)

    def whiten(b):
        def turn(i, _):
            rows = pl.ds(pl.multiple_of(i * 128, 128), 128)
            rows2 = pl.ds(pl.multiple_of(SEGS + i * 128, 128), 128)
            for h in range(2):
                cols = slice(h * PAIR, (h + 1) * PAIR)
                inv = inv_own[b, 0:1, cols]
                re = (raw[h, b, 0, rows, :].astype(f32) * inv).astype(bf)
                im = (raw[h, b, 1, rows, :].astype(f32) * inv).astype(bf)
                white[h, b, 0, rows, :] = re
                white[h, b, 1, rows, :] = im
                re, im = re.T, im.T
                lhs[b, 0, cols, rows] = re
                lhs[b, 0, cols, rows2] = im
                lhs[b, 1, cols, rows] = -im
                lhs[b, 1, cols, rows2] = re
            return 0

        lax.fori_loop(0, SEGS // 128, turn, 0)

    def half_gram(b, group, part, rhs):
        res = jnp.dot(lhs[b, part], rhs, preferred_element_type=f32) * SCALE
        res = res.astype(bf)
        for q in range(2):
            for a in range(NBLK):
                stage[b, group, q, a, part] = res[a * BLK:(a + 1) * BLK, q * BLK:(q + 1) * BLK]

    def out_copy(b, group):
        return pltpu.make_async_copy(
            stage.at[b, group], g_hbm.at[pl.ds(2 + 2 * group, 2), b], out_sem.at[b, group])

    def own_grams(b, pair):
        def part_of(part, _):
            half_gram(b, OWN0 + pair, part, white[pair, b].reshape(2 * SEGS, 2 * BLK))
            return 0

        lax.fori_loop(0, 2, part_of, 0)
        out_copy(b, OWN0 + pair).start()

    whiten(0)
    reduce_step(2)
    whiten(1)
    reduce_step(3)
    halo_start(1, 0)
    own_grams(0, 0)
    reduce_step(4)
    own_grams(0, 1)
    reduce_step(5)
    halo_start(1, 1)
    own_grams(1, 0)
    reduce_step(6)
    own_grams(1, 1)
    for k in range(2):
        ring_copy(0, 7, k).wait_recv()
    xsend[0:128] = mine[z] + ring[0, 8] + ring[1, 7]

    x_copies = [
        remote(xsend, xrecv.at[o], x_s.at[o], x_r.at[o], fq, peers[o]) for o in range(3)
    ]
    for c in x_copies:
        c.start()

    def gram_copy(b, side, n):
        return remote(gsend.at[b, side, n], grecv.at[b, side, n], gs_s.at[b, side, n],
                      gs_r.at[b, side, n], fq, right if side == 0 else left)

    def halo_grams(b):
        for side, group in ((0, LEFT), (1, RIGHT)):
            for part in range(2):
                halo_copy(b, side, part).wait_recv()

            def scale(i, _, side=side):
                rows = pl.ds(i * 64, 64)
                for part in range(2):
                    v = halo[side, b, part, rows, :].astype(f32) * inv_halo[side, b, 0:1, :]
                    halo[side, b, part, rows, :] = v.astype(bf)
                return 0

            lax.fori_loop(0, SEGS // 64, scale, 0)

            def part_of(part, _, side=side, group=group):
                half_gram(b, group, part, halo[side, b].reshape(2 * SEGS, 2 * BLK))
                return 0

            lax.fori_loop(0, 2, part_of, 0)
            out_copy(b, group).start()
            if side == 1:
                for n, (la, lb) in enumerate(TO_RIGHT):
                    gsend[b, 0, n, 0] = stage[b, RIGHT, lb, la, 0].T
                    gsend[b, 0, n, 1] = -stage[b, RIGHT, lb, la, 1].T
                    gram_copy(b, 0, n).start()
            else:
                for n, (la, lb) in enumerate(TO_LEFT):
                    gsend[b, 1, n, 0] = stage[b, LEFT, la - 2, lb, 0].T
                    gsend[b, 1, n, 1] = -stage[b, LEFT, la - 2, lb, 1].T
                    gram_copy(b, 1, n).start()

    inv_copy(0).wait_recv()
    inv_copy(1).wait_recv()
    halo_grams(0)

    for c in x_copies:
        c.wait_recv()
    full[z] = xsend[...] + xrecv[0] + xrecv[1] + xrecv[2]

    def ag_copy(way, s, k):
        rows = pl.ds(0, 64) if k == 0 else pl.ds(64, 80)
        c = lax.rem(z + NZ - s, NZ) if way == 0 else lax.rem(z + s, NZ)
        return remote(full.at[c, rows], full.at[c, rows], ag_s.at[way, s, k], ag_r.at[way, s, k],
                      fq, z_up if way == 0 else z_dn)

    for k in range(2):
        for way in range(2):
            ag_copy(way, 0, k).start()

    def gather_step(s, _):
        for k in range(2):
            ag_copy(0, s, k).wait_recv()

            @pl.when(s < 7)
            def _():
                ag_copy(0, s + 1, k).start()
                ag_copy(1, s, k).wait_recv()

            @pl.when(s < 6)
            def _():
                ag_copy(1, s + 1, k).start()
        return 0

    lax.fori_loop(0, 2, gather_step, 0)
    halo_grams(1)
    lax.fori_loop(2, 8, gather_step, 0)

    for s in range(8):
        for k in range(2):
            ring_copy(0, s, k).wait_send()
            if s < 7:
                ring_copy(1, s, k).wait_send()
    for b in range(BINS):
        for side in range(2):
            for part in range(2):
                halo_copy(b, side, part).wait_send()

    tail = full[0, 128:144, :].astype(f32)
    for c in range(1, NZ):
        tail = tail + full[c, 128:144, :].astype(f32)
    for b in range(BINS):
        inv = tail[b * 3:b * 3 + 1] + tail[b * 3 + 1:b * 3 + 2] + tail[b * 3 + 2:b * 3 + 3]

        def scale(i, _, b=b, inv=inv):
            c = b * 8 + i // 2
            rows = pl.ds(pl.multiple_of(lax.rem(i, 2) * 64, 64), 64)
            mine[c, rows, :] = (full[c, rows, :].astype(f32) * inv).astype(bf)
            return 0

        lax.fori_loop(0, 16, scale, 0)

        def part_of(part, _, b=b):
            half_gram(b, REFS, part, mine[b * 8:b * 8 + 8].reshape(2 * SEGS, 2 * BLK))
            return 0

        lax.fori_loop(0, 2, part_of, 0)
        out_copy(b, REFS).start()

    def far_copy(b, side, n):
        if side == 0:
            la, lb = TO_RIGHT[n]
            slot, a = la, lb
        else:
            la, lb = TO_LEFT[n]
            slot, a = 10 + lb, la
        return pltpu.make_async_copy(
            grecv.at[b, side, n], g_hbm.at[slot, b, a], far_sem.at[b, side, n])

    for b in range(BINS):
        for side in range(2):
            for n in range(3):
                gram_copy(b, side, n).wait_recv()
                far_copy(b, side, n).start()

    for b in range(BINS):
        for side in range(2):
            for n in range(3):
                gram_copy(b, side, n).wait_send()
                far_copy(b, side, n).wait()
        for group in range(5):
            out_copy(b, group).wait()
    for c in x_copies:
        c.wait_send()
    for side in range(2):
        inv_copy(side).wait_send()

    def drain(s, _):
        for k in range(2):
            ag_copy(0, s, k).wait_send()

            @pl.when(s < 7)
            def _():
                ag_copy(1, s, k).wait_send()
        return 0

    lax.fori_loop(0, 8, drain, 0)


def select_kernel(pairs_ref, g_hbm, pair_out, ref_out, pair_buf, ref_buf, pair_sem, ref_sem):
    base = lax.axis_index("fibre") * NBLK
    copies = []
    for a in range(NBLK):
        for p in range(NP):
            e = pairs_ref[a, p] - base + NBLK
            slot = jnp.where(e >= 10, e + 2, e)
            copies.append((
                pltpu.make_async_copy(g_hbm.at[slot, :, a], pair_buf.at[a, p], pair_sem.at[0, a, p]),
                pltpu.make_async_copy(pair_buf.at[a, p], pair_out.at[:, a, p], pair_sem.at[1, a, p])))
    for r in range(2):
        copies.append((
            pltpu.make_async_copy(g_hbm.at[10 + r], ref_buf.at[r], ref_sem.at[0, r]),
            pltpu.make_async_copy(ref_buf.at[r], ref_out.at[:, :, r], ref_sem.at[1, r])))
    for c, _ in copies:
        c.start()
    for c, d in copies:
        c.wait()
        d.start()
    for _, d in copies:
        d.wait()


def body(spectra, pairs, refs):
    bf = jnp.bfloat16
    smem = pl.BlockSpec(memory_space=pltpu.SMEM)
    hbm = pl.BlockSpec(memory_space=pl.ANY)
    dma = pltpu.SemaphoreType.DMA
    grams = pl.pallas_call(
        kernel,
        out_shape=jax.ShapeDtypeStruct((SLOTS, BINS, NBLK, 2, BLK, BLK), bf),
        in_specs=[smem, hbm],
        out_specs=hbm,
        scratch_shapes=[
            pltpu.VMEM((2, BINS, 2, SEGS, PAIR), bf),
            pltpu.VMEM((2, BINS, 2, SEGS, PAIR), bf),
            pltpu.VMEM((BINS, 2, CHAN, 2 * SEGS), bf),
            pltpu.VMEM((2, BINS, 2, SEGS, 2 * BLK), bf),
            pltpu.VMEM((NZ, 128, 2 * BLK), bf),
            pltpu.VMEM((2, 9, 128, 2 * BLK), bf),
            pltpu.VMEM((144, 2 * BLK), bf),
            pltpu.VMEM((3, 144, 2 * BLK), bf),
            pltpu.VMEM((NZ, 144, 2 * BLK), bf),
            pltpu.VMEM((BINS, 5, 2, NBLK, 2, BLK, BLK), bf),
            pltpu.VMEM((BINS, 2, 3, 2, BLK, BLK), bf),
            pltpu.VMEM((BINS, 2, 3, 2, BLK, BLK), bf),
            pltpu.VMEM((BINS, 8, CHAN), jnp.float32),
            pltpu.VMEM((2, 8, CHAN), jnp.float32),
            pltpu.VMEM((BINS, 8, CHAN), jnp.float32),
            pltpu.VMEM((2, BINS, 8, 2 * BLK), jnp.float32),
            pltpu.VMEM((2, 16, CHAN), bf),
            dma((BINS, 2)),
            dma((2,)), dma((2,)),
            dma((2, BINS, 2)), dma((2, BINS, 2)),
            dma((2, 8, 2)), dma((2, 8, 2)),
            dma((3,)), dma((3,)),
            dma((2, 8, 2)), dma((2, 8, 2)),
            dma((BINS, 2, 3)), dma((BINS, 2, 3)),
            dma((2,)), dma((2,)),
            dma((BINS, 5)),
            dma((BINS, 2, 3)),
        ],
        compiler_params=pltpu.CompilerParams(
            collective_id=0, has_side_effects=True, vmem_limit_bytes=60 * 1024 * 1024),
        cost_estimate=pl.CostEstimate(
            flops=5_400_000_000, bytes_accessed=8 * 1024 * 1024, transcendentals=1024),
        name="grams",
    )(refs, spectra)
    return pl.pallas_call(
        select_kernel,
        out_shape=(
            jax.ShapeDtypeStruct((BINS, NBLK, NP, 2, BLK, BLK), bf),
            jax.ShapeDtypeStruct((BINS, NBLK, 2, 2, BLK, BLK), bf),
        ),
        in_specs=[smem, hbm],
        out_specs=(hbm, hbm),
        scratch_shapes=[
            pltpu.VMEM((NBLK, NP, BINS, 2, BLK, BLK), bf),
            pltpu.VMEM((2, BINS, NBLK, 2, BLK, BLK), bf),
            dma((2, NBLK, NP)), dma((2, 2)),
        ],
        compiler_params=pltpu.CompilerParams(vmem_limit_bytes=60 * 1024 * 1024),
        cost_estimate=pl.CostEstimate(
            flops=0, bytes_accessed=6 * 1024 * 1024, transcendentals=0),
        name="select",
    )(pairs, grams)


def solution(mesh):
    return jax.shard_map(
        body,
        mesh=mesh,
        in_specs=(P("freq", None, None, "fibre"), P("fibre", None), P()),
        out_specs=(
            P("freq", "fibre", None, None, None, None),
            P("freq", "fibre", None, None, None, None),
        ),
        check_vma=False,
    )
```

```python
import math

import jax
import jax.numpy as jnp
from jax import lax
from jax.experimental import pallas as pl
from jax.experimental.pallas import tpu as pltpu
from jax.sharding import PartitionSpec as P

BLK = 128
NP = 4
SEGS = 512
EPS = 1e-06
BINS = 2
NBLK = 4
CHAN = NBLK * BLK
PAIR = 2 * BLK
NX = 4
NZ = 16
NF = 8
NFIB = NX * NZ
SCALE = 1.0 / math.sqrt(SEGS)
MESH = pl.DeviceIdType.MESH
TO_RIGHT = ((0, 0), (1, 0), (1, 1))
TO_LEFT = ((2, 2), (3, 2), (3, 3))
SLOTS = 14
LEFT, OWN0, OWN1, RIGHT, REFS = range(5)


def kernel(
    refs_ref, spec_hbm, g_hbm,
    raw, white, lhs, halo, mine, ring, xsend, xrecv, full, stage, gsend, grecv,
    psend, precv, inv_own, inv_halo, mask_ref,
    load_sem, pow_s, pow_r, halo_s, halo_r, ring_s, ring_r, x_s, x_r, ag_s, ag_r,
    gs_s, gs_r, inv_s, inv_r, out_sem, far_sem,
):
    f32, bf = jnp.float32, jnp.bfloat16
    fq = lax.axis_index("freq")
    fb = lax.axis_index("fibre")
    x = lax.rem(fb, NX)
    z = fb // NX
    f_up, f_dn = lax.rem(fq + 1, NF), lax.rem(fq + NF - 1, NF)
    right, left = lax.rem(fb + 1, NFIB), lax.rem(fb + NFIB - 1, NFIB)
    z_up, z_dn = lax.rem(fb + NX, NFIB), lax.rem(fb + NFIB - NX, NFIB)
    peers = [z * NX + lax.rem(x + o, NX) for o in (1, 2, 3)]

    def remote(src, dst, s_sem, r_sem, f, d):
        return pltpu.make_async_remote_copy(
            src, dst, s_sem, r_sem, device_id=(f, d), device_id_type=MESH)

    loads = [
        pltpu.make_async_copy(
            spec_hbm.at[b, :, :, pl.ds(h * PAIR, PAIR)], raw.at[h, b], load_sem.at[b, h])
        for b in range(BINS) for h in range(2)
    ]
    for c in loads:
        c.start()

    barrier = pltpu.get_barrier_semaphore()
    for f in (f_up, f_dn):
        pl.semaphore_signal(barrier, inc=1, device_id=(f, fb), device_id_type=MESH)
    for d in [right, left, z_up, z_dn] + peers:
        pl.semaphore_signal(barrier, inc=1, device_id=(fq, d), device_id_type=MESH)

    block = fb * NBLK + lax.broadcasted_iota(jnp.int32, (16, CHAN), 1) // BLK
    for r in range(2):
        mask_ref[r] = jnp.where(block == refs_ref[r], 1.0, 0.0).astype(bf)

    def gather_lanes(t):
        return (t[..., :BLK] + t[..., BLK:2 * BLK]) + (t[..., 2 * BLK:3 * BLK] + t[..., 3 * BLK:])

    def gather_two(t):
        return t[..., :BLK] + t[..., BLK:]

    for b in range(BINS):
        loads[2 * b].wait()
        loads[2 * b + 1].wait()

        def pick(i, _, b=b):
            for part in range(2):
                v = [raw[h, b, part, pl.ds(i * 128, 128), :].reshape(8, 16, PAIR) for h in range(2)]
                for r in range(2):
                    m = mask_ref[r]
                    t = gather_two(v[0] * m[None, :, :PAIR]) + gather_two(v[1] * m[None, :, PAIR:])
                    mine[b * 8 + part * 4 + i, :, r * BLK:(r + 1) * BLK] = t.reshape(128, BLK)
            return 0

        lax.fori_loop(0, 4, pick, 0)

    def ring_copy(way, s, k):
        rows = pl.ds(k * 64, 64)
        src = mine.at[lax.rem(z + 8, NZ) if way == 0 else lax.rem(z + NZ - 7, NZ), rows]
        if not (isinstance(s, int) and s == 0):
            src = ring.at[way, s, rows]
        return remote(src, ring.at[way, s + 1, rows], ring_s.at[way, s, k], ring_r.at[way, s, k],
                      fq, z_up if way == 0 else z_dn)

    def halo_copy(b, side, part, half):
        rows = pl.ds(half * 256, 256)
        return remote(raw.at[1 - side, b, part, rows], halo.at[side, b, part, rows],
                      halo_s.at[side, b, part, half], halo_r.at[side, b, part, half],
                      fq, right if side == 0 else left)

    def inv_copy(side):
        cols = pl.ds(2 * BLK, 2 * BLK) if side == 0 else pl.ds(0, 2 * BLK)
        return remote(inv_own.at[:, :, cols], inv_halo.at[side], inv_s.at[side], inv_r.at[side],
                      fq, right if side == 0 else left)

    pl.semaphore_wait(barrier, 9)
    for k in range(2):
        for way in range(2):
            ring_copy(way, 0, k).start()

    def halo_start(piece):
        for side in range(2):
            halo_copy(piece // 4, side, piece // 2 % 2, piece % 2).start()

    halo_start(0)

    def reduce_step(s):
        for k in range(2):
            rows = pl.ds(k * 64, 64)
            ring_copy(0, s, k).wait_recv()
            ring[0, s + 1, rows] = ring[0, s + 1, rows] + mine[lax.rem(z + 7 - s + NZ, NZ), rows]
            if s < 7:
                ring_copy(0, s + 1, k).start()
            if s < 7:
                ring_copy(1, s, k).wait_recv()
            if s < 6:
                ring[1, s + 1, rows] = ring[1, s + 1, rows] + mine[lax.rem(z + NZ - 6 + s, NZ), rows]
                ring_copy(1, s + 1, k).start()

    for b in range(BINS):
        def add(i, acc, b=b):
            for part in range(2):
                v = [raw[h, b, part, pl.ds(i * 64, 64), :].astype(f32) for h in range(2)]
                acc = [a + jnp.sum((w * w).reshape(8, 8, PAIR), axis=0) for a, w in zip(acc, v)]
            return acc

        acc = lax.fori_loop(0, SEGS // 64, add, [jnp.zeros((8, PAIR), f32)] * 2)
        psend[b, :, :PAIR] = acc[0]
        psend[b, :, PAIR:] = acc[1]

    up = remote(psend.at[1], precv.at[0], pow_s.at[0], pow_r.at[0], f_up, fb)
    dn = remote(psend.at[0], precv.at[1], pow_s.at[1], pow_r.at[1], f_dn, fb)
    up.start()
    dn.start()
    reduce_step(0)
    halo_start(1)

    def total(v):
        return jnp.sum(v, axis=0, keepdims=True) / SEGS

    p0, p1 = total(psend[0]), total(psend[1])
    up.wait()
    dn.wait()
    below = jnp.where(fq == 0, 0.0, total(precv[0]))
    above = jnp.where(fq == NF - 1, 0.0, total(precv[1]))
    c0 = jnp.where(fq == 0, 2.0, 3.0)
    c1 = jnp.where(fq == NF - 1, 2.0, 3.0)
    smooth = [(below + p0 + p1) / c0, (p0 + p1 + above) / c1]
    row = lax.broadcasted_iota(jnp.int32, (16, BLK), 0)
    for b in range(BINS):
        inv_own[b] = jnp.broadcast_to(1.0 / jnp.sqrt(smooth[b] + EPS), (8, CHAN))
    inv_copy(0).start()
    inv_copy(1).start()
    for r in range(2):
        tile = jnp.zeros((16, BLK), f32)
        for b in range(BINS):
            v = gather_lanes(inv_own[b, 0:1, :] * mask_ref[r, 0:1, :].astype(f32))
            for piece in range(3):
                part = v.astype(bf).astype(f32)
                tile = jnp.where(row == b * 3 + piece, jnp.broadcast_to(part, (16, BLK)), tile)
                v = v - part
        xsend[128:144, r * BLK:(r + 1) * BLK] = tile.astype(bf)
    reduce_step(1)
    halo_start(2)

    def whiten(b):
        def turn(i, _):
            rows = pl.ds(pl.multiple_of(i * 128, 128), 128)
            rows2 = pl.ds(pl.multiple_of(SEGS + i * 128, 128), 128)
            for h in range(2):
                cols = slice(h * PAIR, (h + 1) * PAIR)
                inv = inv_own[b, 0:1, cols]
                re = (raw[h, b, 0, rows, :].astype(f32) * inv).astype(bf)
                im = (raw[h, b, 1, rows, :].astype(f32) * inv).astype(bf)
                white[h, b, 0, rows, :] = re
                white[h, b, 1, rows, :] = im
                re, im = re.T, im.T
                lhs[b, 0, cols, rows] = re
                lhs[b, 0, cols, rows2] = im
                lhs[b, 1, cols, rows] = -im
                lhs[b, 1, cols, rows2] = re
            return 0

        lax.fori_loop(0, SEGS // 128, turn, 0)

    def half_gram(b, group, part, rhs):
        res = jnp.dot(lhs[b, part], rhs, preferred_element_type=f32) * SCALE
        res = res.astype(bf)
        for q in range(2):
            for a in range(NBLK):
                stage[b, group, q, a, part] = res[a * BLK:(a + 1) * BLK, q * BLK:(q + 1) * BLK]

    def out_copy(b, group):
        return pltpu.make_async_copy(
            stage.at[b, group], g_hbm.at[pl.ds(2 + 2 * group, 2), b], out_sem.at[b, group])

    def own_grams(b, pair):
        def part_of(part, _):
            half_gram(b, OWN0 + pair, part, white[pair, b].reshape(2 * SEGS, 2 * BLK))
            return 0

        lax.fori_loop(0, 2, part_of, 0)
        out_copy(b, OWN0 + pair).start()

    whiten(0)
    reduce_step(2)
    halo_start(3)
    whiten(1)
    reduce_step(3)
    halo_start(4)
    own_grams(0, 0)
    reduce_step(4)
    halo_start(5)
    own_grams(0, 1)
    reduce_step(5)
    halo_start(6)
    own_grams(1, 0)
    reduce_step(6)
    own_grams(1, 1)
    for k in range(2):
        ring_copy(0, 7, k).wait_recv()
    xsend[0:128] = mine[z] + ring[0, 8] + ring[1, 7]

    x_copies = [
        remote(xsend, xrecv.at[o], x_s.at[o], x_r.at[o], fq, peers[o]) for o in range(3)
    ]
    for c in x_copies:
        c.start()
    halo_start(7)

    def gram_copy(b, side, n):
        return remote(gsend.at[b, side, n], grecv.at[b, side, n], gs_s.at[b, side, n],
                      gs_r.at[b, side, n], fq, right if side == 0 else left)

    def halo_grams(b):
        for side, group in ((0, LEFT), (1, RIGHT)):
            for part in range(2):
                for half in range(2):
                    halo_copy(b, side, part, half).wait_recv()

            def scale(i, _, side=side):
                rows = pl.ds(i * 64, 64)
                for part in range(2):
                    v = halo[side, b, part, rows, :].astype(f32) * inv_halo[side, b, 0:1, :]
                    halo[side, b, part, rows, :] = v.astype(bf)
                return 0

            lax.fori_loop(0, SEGS // 64, scale, 0)

            def part_of(part, _, side=side, group=group):
                half_gram(b, group, part, halo[side, b].reshape(2 * SEGS, 2 * BLK))
                return 0

            lax.fori_loop(0, 2, part_of, 0)
            out_copy(b, group).start()
            if side == 1:
                for n, (la, lb) in enumerate(TO_RIGHT):
                    gsend[b, 0, n, 0] = stage[b, RIGHT, lb, la, 0].T
                    gsend[b, 0, n, 1] = -stage[b, RIGHT, lb, la, 1].T
            else:
                for n, (la, lb) in enumerate(TO_LEFT):
                    gsend[b, 1, n, 0] = stage[b, LEFT, la - 2, lb, 0].T
                    gsend[b, 1, n, 1] = -stage[b, LEFT, la - 2, lb, 1].T

    inv_copy(0).wait_recv()
    inv_copy(1).wait_recv()
    halo_grams(0)

    for c in x_copies:
        c.wait_recv()
    full[z] = xsend[...] + xrecv[0] + xrecv[1] + xrecv[2]

    def ag_copy(way, s, k):
        rows = pl.ds(0, 64) if k == 0 else pl.ds(64, 80)
        c = lax.rem(z + NZ - s, NZ) if way == 0 else lax.rem(z + s, NZ)
        return remote(full.at[c, rows], full.at[c, rows], ag_s.at[way, s, k], ag_r.at[way, s, k],
                      fq, z_up if way == 0 else z_dn)

    for k in range(2):
        for way in range(2):
            ag_copy(way, 0, k).start()

    def gather_step(s):
        for k in range(2):
            ag_copy(0, s, k).wait_recv()

            @pl.when(s < 7)
            def _():
                ag_copy(0, s + 1, k).start()
                ag_copy(1, s, k).wait_recv()

            @pl.when(s < 6)
            def _():
                ag_copy(1, s + 1, k).start()

    def gather_and_send(b, first):
        def step(s, _):
            gather_step(s)
            for side in range(2):
                gram_copy(b, side, s - first).start()
            return 0

        lax.fori_loop(first, first + 3, step, 0)

    def gather_rest(s, _):
        gather_step(s)
        return 0

    gather_and_send(0, 0)
    halo_grams(1)
    gather_and_send(1, 3)
    lax.fori_loop(6, 8, gather_rest, 0)

    for s in range(8):
        for k in range(2):
            ring_copy(0, s, k).wait_send()
            if s < 7:
                ring_copy(1, s, k).wait_send()
    for b in range(BINS):
        for side in range(2):
            for part in range(2):
                for half in range(2):
                    halo_copy(b, side, part, half).wait_send()

    tail = full[0, 128:144, :].astype(f32)
    for c in range(1, NZ):
        tail = tail + full[c, 128:144, :].astype(f32)
    for b in range(BINS):
        inv = tail[b * 3:b * 3 + 1] + tail[b * 3 + 1:b * 3 + 2] + tail[b * 3 + 2:b * 3 + 3]

        def scale(i, _, b=b, inv=inv):
            c = b * 8 + i // 2
            rows = pl.ds(pl.multiple_of(lax.rem(i, 2) * 64, 64), 64)
            mine[c, rows, :] = (full[c, rows, :].astype(f32) * inv).astype(bf)
            return 0

        lax.fori_loop(0, 16, scale, 0)

        def part_of(part, _, b=b):
            half_gram(b, REFS, part, mine[b * 8:b * 8 + 8].reshape(2 * SEGS, 2 * BLK))
            return 0

        lax.fori_loop(0, 2, part_of, 0)
        out_copy(b, REFS).start()

    def far_copy(b, side, n):
        if side == 0:
            la, lb = TO_RIGHT[n]
            slot, a = la, lb
        else:
            la, lb = TO_LEFT[n]
            slot, a = 10 + lb, la
        return pltpu.make_async_copy(
            grecv.at[b, side, n], g_hbm.at[slot, b, a], far_sem.at[b, side, n])

    for b in range(BINS):
        for side in range(2):
            for n in range(3):
                gram_copy(b, side, n).wait_recv()
                far_copy(b, side, n).start()

    for b in range(BINS):
        for side in range(2):
            for n in range(3):
                gram_copy(b, side, n).wait_send()
                far_copy(b, side, n).wait()
        for group in range(5):
            out_copy(b, group).wait()
    for c in x_copies:
        c.wait_send()
    for side in range(2):
        inv_copy(side).wait_send()

    def drain(s, _):
        for k in range(2):
            ag_copy(0, s, k).wait_send()

            @pl.when(s < 7)
            def _():
                ag_copy(1, s, k).wait_send()
        return 0

    lax.fori_loop(0, 8, drain, 0)


def select_kernel(pairs_ref, g_hbm, pair_out, ref_out, pair_buf, ref_buf, pair_sem, ref_sem):
    base = lax.axis_index("fibre") * NBLK
    copies = []
    for a in range(NBLK):
        for p in range(NP):
            e = pairs_ref[a, p] - base + NBLK
            slot = jnp.where(e >= 10, e + 2, e)
            copies.append((
                pltpu.make_async_copy(g_hbm.at[slot, :, a], pair_buf.at[a, p], pair_sem.at[0, a, p]),
                pltpu.make_async_copy(pair_buf.at[a, p], pair_out.at[:, a, p], pair_sem.at[1, a, p])))
    for r in range(2):
        copies.append((
            pltpu.make_async_copy(g_hbm.at[10 + r], ref_buf.at[r], ref_sem.at[0, r]),
            pltpu.make_async_copy(ref_buf.at[r], ref_out.at[:, :, r], ref_sem.at[1, r])))
    for c, _ in copies:
        c.start()
    for c, d in copies:
        c.wait()
        d.start()
    for _, d in copies:
        d.wait()


def body(spectra, pairs, refs):
    bf = jnp.bfloat16
    smem = pl.BlockSpec(memory_space=pltpu.SMEM)
    hbm = pl.BlockSpec(memory_space=pl.ANY)
    dma = pltpu.SemaphoreType.DMA
    grams = pl.pallas_call(
        kernel,
        out_shape=jax.ShapeDtypeStruct((SLOTS, BINS, NBLK, 2, BLK, BLK), bf),
        in_specs=[smem, hbm],
        out_specs=hbm,
        scratch_shapes=[
            pltpu.VMEM((2, BINS, 2, SEGS, PAIR), bf),
            pltpu.VMEM((2, BINS, 2, SEGS, PAIR), bf),
            pltpu.VMEM((BINS, 2, CHAN, 2 * SEGS), bf),
            pltpu.VMEM((2, BINS, 2, SEGS, 2 * BLK), bf),
            pltpu.VMEM((NZ, 128, 2 * BLK), bf),
            pltpu.VMEM((2, 9, 128, 2 * BLK), bf),
            pltpu.VMEM((144, 2 * BLK), bf),
            pltpu.VMEM((3, 144, 2 * BLK), bf),
            pltpu.VMEM((NZ, 144, 2 * BLK), bf),
            pltpu.VMEM((BINS, 5, 2, NBLK, 2, BLK, BLK), bf),
            pltpu.VMEM((BINS, 2, 3, 2, BLK, BLK), bf),
            pltpu.VMEM((BINS, 2, 3, 2, BLK, BLK), bf),
            pltpu.VMEM((BINS, 8, CHAN), jnp.float32),
            pltpu.VMEM((2, 8, CHAN), jnp.float32),
            pltpu.VMEM((BINS, 8, CHAN), jnp.float32),
            pltpu.VMEM((2, BINS, 8, 2 * BLK), jnp.float32),
            pltpu.VMEM((2, 16, CHAN), bf),
            dma((BINS, 2)),
            dma((2,)), dma((2,)),
            dma((2, BINS, 2, 2)), dma((2, BINS, 2, 2)),
            dma((2, 8, 2)), dma((2, 8, 2)),
            dma((3,)), dma((3,)),
            dma((2, 8, 2)), dma((2, 8, 2)),
            dma((BINS, 2, 3)), dma((BINS, 2, 3)),
            dma((2,)), dma((2,)),
            dma((BINS, 5)),
            dma((BINS, 2, 3)),
        ],
        compiler_params=pltpu.CompilerParams(
            collective_id=0, has_side_effects=True, vmem_limit_bytes=60 * 1024 * 1024),
        cost_estimate=pl.CostEstimate(
            flops=5_400_000_000, bytes_accessed=8 * 1024 * 1024, transcendentals=1024),
        name="grams",
    )(refs, spectra)
    return pl.pallas_call(
        select_kernel,
        out_shape=(
            jax.ShapeDtypeStruct((BINS, NBLK, NP, 2, BLK, BLK), bf),
            jax.ShapeDtypeStruct((BINS, NBLK, 2, 2, BLK, BLK), bf),
        ),
        in_specs=[smem, hbm],
        out_specs=(hbm, hbm),
        scratch_shapes=[
            pltpu.VMEM((NBLK, NP, BINS, 2, BLK, BLK), bf),
            pltpu.VMEM((2, BINS, NBLK, 2, BLK, BLK), bf),
            dma((2, NBLK, NP)), dma((2, 2)),
        ],
        compiler_params=pltpu.CompilerParams(vmem_limit_bytes=60 * 1024 * 1024),
        cost_estimate=pl.CostEstimate(
            flops=0, bytes_accessed=6 * 1024 * 1024, transcendentals=0),
        name="select",
    )(pairs, grams)


def solution(mesh):
    return jax.shard_map(
        body,
        mesh=mesh,
        in_specs=(P("freq", None, None, "fibre"), P("fibre", None), P()),
        out_specs=(
            P("freq", "fibre", None, None, None, None),
            P("freq", "fibre", None, None, None, None),
        ),
        check_vma=False,
    )
```

```python
import math

import jax
import jax.numpy as jnp
from jax import lax
from jax.experimental import pallas as pl
from jax.experimental.pallas import tpu as pltpu
from jax.sharding import PartitionSpec as P

BLK = 128
NP = 4
SEGS = 512
EPS = 1e-06
BINS = 2
NBLK = 4
CHAN = NBLK * BLK
PAIR = 2 * BLK
NX = 4
NZ = 16
NF = 8
NFIB = NX * NZ
SCALE = 1.0 / math.sqrt(SEGS)
MESH = pl.DeviceIdType.MESH
TO_RIGHT = ((0, 0), (1, 0), (1, 1))
TO_LEFT = ((2, 2), (3, 2), (3, 3))
SLOTS = 14
LEFT, OWN0, OWN1, RIGHT, REFS = range(5)
PIECES = (
    (0, 0, 0, 128), (0, 0, 128, 256), (0, 0, 384, 128),
    (0, 1, 0, 256), (0, 1, 256, 128), (0, 1, 384, 128),
    (1, 0, 0, 256), (1, 0, 256, 128), (1, 0, 384, 128),
    (1, 1, 0, 128), (1, 1, 128, 128), (1, 1, 256, 256),
)


def kernel(
    refs_ref, spec_hbm, g_hbm,
    raw, white, lhs, halo, mine, ring, xsend, xrecv, full, stage, gsend, grecv,
    psend, precv, inv_own, inv_halo, mask_ref,
    load_sem, pow_s, pow_r, halo_s, halo_r, ring_s, ring_r, x_s, x_r, ag_s, ag_r,
    gs_s, gs_r, inv_s, inv_r, out_sem, far_sem,
):
    f32, bf = jnp.float32, jnp.bfloat16
    fq = lax.axis_index("freq")
    fb = lax.axis_index("fibre")
    x = lax.rem(fb, NX)
    z = fb // NX
    f_up, f_dn = lax.rem(fq + 1, NF), lax.rem(fq + NF - 1, NF)
    right, left = lax.rem(fb + 1, NFIB), lax.rem(fb + NFIB - 1, NFIB)
    z_up, z_dn = lax.rem(fb + NX, NFIB), lax.rem(fb + NFIB - NX, NFIB)
    peers = [z * NX + lax.rem(x + o, NX) for o in (1, 2, 3)]

    def remote(src, dst, s_sem, r_sem, f, d):
        return pltpu.make_async_remote_copy(
            src, dst, s_sem, r_sem, device_id=(f, d), device_id_type=MESH)

    loads = [
        pltpu.make_async_copy(
            spec_hbm.at[b, :, :, pl.ds(h * PAIR, PAIR)], raw.at[h, b], load_sem.at[b, h])
        for b in range(BINS) for h in range(2)
    ]
    for c in loads:
        c.start()

    barrier = pltpu.get_barrier_semaphore()
    for f in (f_up, f_dn):
        pl.semaphore_signal(barrier, inc=1, device_id=(f, fb), device_id_type=MESH)
    for d in [right, left, z_up, z_dn] + peers:
        pl.semaphore_signal(barrier, inc=1, device_id=(fq, d), device_id_type=MESH)

    block = fb * NBLK + lax.broadcasted_iota(jnp.int32, (16, CHAN), 1) // BLK
    for r in range(2):
        mask_ref[r] = jnp.where(block == refs_ref[r], 1.0, 0.0).astype(bf)

    def gather_lanes(t):
        return (t[..., :BLK] + t[..., BLK:2 * BLK]) + (t[..., 2 * BLK:3 * BLK] + t[..., 3 * BLK:])

    def gather_two(t):
        return t[..., :BLK] + t[..., BLK:]

    for b in range(BINS):
        loads[2 * b].wait()
        loads[2 * b + 1].wait()

        def pick(i, _, b=b):
            for part in range(2):
                v = [raw[h, b, part, pl.ds(i * 128, 128), :].reshape(8, 16, PAIR) for h in range(2)]
                for r in range(2):
                    m = mask_ref[r]
                    t = gather_two(v[0] * m[None, :, :PAIR]) + gather_two(v[1] * m[None, :, PAIR:])
                    mine[b * 8 + part * 4 + i, :, r * BLK:(r + 1) * BLK] = t.reshape(128, BLK)
            return 0

        lax.fori_loop(0, 4, pick, 0)

    def ring_copy(way, s, k):
        rows = pl.ds(k * 64, 64)
        src = mine.at[lax.rem(z + 8, NZ) if way == 0 else lax.rem(z + NZ - 7, NZ), rows]
        if not (isinstance(s, int) and s == 0):
            src = ring.at[way, s, rows]
        return remote(src, ring.at[way, s + 1, rows], ring_s.at[way, s, k], ring_r.at[way, s, k],
                      fq, z_up if way == 0 else z_dn)

    def halo_copy(n, side):
        b, part, first, size = PIECES[n]
        rows = pl.ds(first, size)
        return remote(raw.at[1 - side, b, part, rows], halo.at[side, b, part, rows],
                      halo_s.at[side, n], halo_r.at[side, n], fq, right if side == 0 else left)

    def inv_copy(side):
        cols = pl.ds(2 * BLK, 2 * BLK) if side == 0 else pl.ds(0, 2 * BLK)
        return remote(inv_own.at[:, :, cols], inv_halo.at[side], inv_s.at[side], inv_r.at[side],
                      fq, right if side == 0 else left)

    pl.semaphore_wait(barrier, 9)
    for k in range(2):
        for way in range(2):
            ring_copy(way, 0, k).start()

    def halo_start(piece):
        for side in range(2):
            halo_copy(piece, side).start()

    halo_start(0)

    def reduce_step(s):
        for k in range(2):
            rows = pl.ds(k * 64, 64)
            ring_copy(0, s, k).wait_recv()
            ring[0, s + 1, rows] = ring[0, s + 1, rows] + mine[lax.rem(z + 7 - s + NZ, NZ), rows]
            if s < 7:
                ring_copy(0, s + 1, k).start()
            if s < 7:
                ring_copy(1, s, k).wait_recv()
            if s < 6:
                ring[1, s + 1, rows] = ring[1, s + 1, rows] + mine[lax.rem(z + NZ - 6 + s, NZ), rows]
                ring_copy(1, s + 1, k).start()

    for b in range(BINS):
        def add(i, acc, b=b):
            for part in range(2):
                v = [raw[h, b, part, pl.ds(i * 64, 64), :].astype(f32) for h in range(2)]
                acc = [a + jnp.sum((w * w).reshape(8, 8, PAIR), axis=0) for a, w in zip(acc, v)]
            return acc

        acc = lax.fori_loop(0, SEGS // 64, add, [jnp.zeros((8, PAIR), f32)] * 2)
        psend[b, :, :PAIR] = acc[0]
        psend[b, :, PAIR:] = acc[1]

    up = remote(psend.at[1], precv.at[0], pow_s.at[0], pow_r.at[0], f_up, fb)
    dn = remote(psend.at[0], precv.at[1], pow_s.at[1], pow_r.at[1], f_dn, fb)
    up.start()
    dn.start()
    reduce_step(0)
    halo_start(1)

    def total(v):
        return jnp.sum(v, axis=0, keepdims=True) / SEGS

    p0, p1 = total(psend[0]), total(psend[1])
    up.wait()
    dn.wait()
    below = jnp.where(fq == 0, 0.0, total(precv[0]))
    above = jnp.where(fq == NF - 1, 0.0, total(precv[1]))
    c0 = jnp.where(fq == 0, 2.0, 3.0)
    c1 = jnp.where(fq == NF - 1, 2.0, 3.0)
    smooth = [(below + p0 + p1) / c0, (p0 + p1 + above) / c1]
    row = lax.broadcasted_iota(jnp.int32, (16, BLK), 0)
    for b in range(BINS):
        inv_own[b] = jnp.broadcast_to(1.0 / jnp.sqrt(smooth[b] + EPS), (8, CHAN))
    inv_copy(0).start()
    inv_copy(1).start()
    for r in range(2):
        tile = jnp.zeros((16, BLK), f32)
        for b in range(BINS):
            v = gather_lanes(inv_own[b, 0:1, :] * mask_ref[r, 0:1, :].astype(f32))
            for piece in range(3):
                part = v.astype(bf).astype(f32)
                tile = jnp.where(row == b * 3 + piece, jnp.broadcast_to(part, (16, BLK)), tile)
                v = v - part
        xsend[128:144, r * BLK:(r + 1) * BLK] = tile.astype(bf)
    reduce_step(1)
    halo_start(2)

    def whiten(b):
        def turn(i, _):
            rows = pl.ds(pl.multiple_of(i * 128, 128), 128)
            rows2 = pl.ds(pl.multiple_of(SEGS + i * 128, 128), 128)
            for h in range(2):
                cols = slice(h * PAIR, (h + 1) * PAIR)
                inv = inv_own[b, 0:1, cols]
                re = (raw[h, b, 0, rows, :].astype(f32) * inv).astype(bf)
                im = (raw[h, b, 1, rows, :].astype(f32) * inv).astype(bf)
                white[h, b, 0, rows, :] = re
                white[h, b, 1, rows, :] = im
                re, im = re.T, im.T
                lhs[b, 0, cols, rows] = re
                lhs[b, 0, cols, rows2] = im
                lhs[b, 1, cols, rows] = -im
                lhs[b, 1, cols, rows2] = re
            return 0

        lax.fori_loop(0, SEGS // 128, turn, 0)

    def half_gram(b, group, part, rhs):
        res = jnp.dot(lhs[b, part], rhs, preferred_element_type=f32) * SCALE
        res = res.astype(bf)
        for q in range(2):
            for a in range(NBLK):
                stage[b, group, q, a, part] = res[a * BLK:(a + 1) * BLK, q * BLK:(q + 1) * BLK]

    def out_copy(b, group):
        return pltpu.make_async_copy(
            stage.at[b, group], g_hbm.at[pl.ds(2 + 2 * group, 2), b], out_sem.at[b, group])

    def own_grams(b, pair):
        def part_of(part, _):
            half_gram(b, OWN0 + pair, part, white[pair, b].reshape(2 * SEGS, 2 * BLK))
            return 0

        lax.fori_loop(0, 2, part_of, 0)
        out_copy(b, OWN0 + pair).start()

    whiten(0)
    reduce_step(2)
    halo_start(3)
    whiten(1)
    reduce_step(3)
    halo_start(4)
    own_grams(0, 0)
    reduce_step(4)
    halo_start(5)
    own_grams(0, 1)
    reduce_step(5)
    halo_start(6)
    own_grams(1, 0)
    reduce_step(6)
    halo_start(7)
    own_grams(1, 1)
    for k in range(2):
        ring_copy(0, 7, k).wait_recv()
    xsend[0:128] = mine[z] + ring[0, 8] + ring[1, 7]

    x_copies = [
        remote(xsend, xrecv.at[o], x_s.at[o], x_r.at[o], fq, peers[o]) for o in range(3)
    ]
    for c in x_copies:
        c.start()

    def gram_copy(b, side, n):
        return remote(gsend.at[b, side, n], grecv.at[b, side, n], gs_s.at[b, side, n],
                      gs_r.at[b, side, n], fq, right if side == 0 else left)

    def halo_grams(b):
        for side, group in ((0, LEFT), (1, RIGHT)):
            for n in range(b * 6, b * 6 + 6):
                halo_copy(n, side).wait_recv()

            def scale(i, _, side=side):
                rows = pl.ds(i * 64, 64)
                for part in range(2):
                    v = halo[side, b, part, rows, :].astype(f32) * inv_halo[side, b, 0:1, :]
                    halo[side, b, part, rows, :] = v.astype(bf)
                return 0

            lax.fori_loop(0, SEGS // 64, scale, 0)

            def part_of(part, _, side=side, group=group):
                half_gram(b, group, part, halo[side, b].reshape(2 * SEGS, 2 * BLK))
                return 0

            lax.fori_loop(0, 2, part_of, 0)
            out_copy(b, group).start()
            if side == 1:
                for n, (la, lb) in enumerate(TO_RIGHT):
                    gsend[b, 0, n, 0] = stage[b, RIGHT, lb, la, 0].T
                    gsend[b, 0, n, 1] = -stage[b, RIGHT, lb, la, 1].T
            else:
                for n, (la, lb) in enumerate(TO_LEFT):
                    gsend[b, 1, n, 0] = stage[b, LEFT, la - 2, lb, 0].T
                    gsend[b, 1, n, 1] = -stage[b, LEFT, la - 2, lb, 1].T

    inv_copy(0).wait_recv()
    inv_copy(1).wait_recv()
    halo_grams(0)

    for c in x_copies:
        c.wait_recv()
    full[z] = xsend[...] + xrecv[0] + xrecv[1] + xrecv[2]

    def ag_copy(way, s, k):
        rows = pl.ds(0, 64) if k == 0 else pl.ds(64, 80)
        c = lax.rem(z + NZ - s, NZ) if way == 0 else lax.rem(z + s, NZ)
        return remote(full.at[c, rows], full.at[c, rows], ag_s.at[way, s, k], ag_r.at[way, s, k],
                      fq, z_up if way == 0 else z_dn)

    for k in range(2):
        for way in range(2):
            ag_copy(way, 0, k).start()

    def gather_step(s):
        for k in range(2):
            ag_copy(0, s, k).wait_recv()

            @pl.when(s < 7)
            def _():
                ag_copy(0, s + 1, k).start()
                ag_copy(1, s, k).wait_recv()

            @pl.when(s < 6)
            def _():
                ag_copy(1, s + 1, k).start()

    def gather_and_send(b, first):
        def step(s, _):
            gather_step(s)
            for side in range(2):
                gram_copy(b, side, s - first).start()
            return 0

        lax.fori_loop(first, first + 3, step, 0)

    for s in range(2):
        gather_step(s)
        halo_start(8 + s)
    for s in range(2, 4):
        gather_step(s)
        halo_start(8 + s)
        for side in range(2):
            gram_copy(0, side, s - 2).start()
    gather_step(4)
    for side in range(2):
        gram_copy(0, side, 2).start()
    halo_grams(1)
    gather_and_send(1, 5)

    for s in range(8):
        for k in range(2):
            ring_copy(0, s, k).wait_send()
            if s < 7:
                ring_copy(1, s, k).wait_send()
    for n in range(12):
        for side in range(2):
            halo_copy(n, side).wait_send()

    tail = full[0, 128:144, :].astype(f32)
    for c in range(1, NZ):
        tail = tail + full[c, 128:144, :].astype(f32)
    for b in range(BINS):
        inv = tail[b * 3:b * 3 + 1] + tail[b * 3 + 1:b * 3 + 2] + tail[b * 3 + 2:b * 3 + 3]

        def scale(i, _, b=b, inv=inv):
            c = b * 8 + i // 2
            rows = pl.ds(pl.multiple_of(lax.rem(i, 2) * 64, 64), 64)
            mine[c, rows, :] = (full[c, rows, :].astype(f32) * inv).astype(bf)
            return 0

        lax.fori_loop(0, 16, scale, 0)

        def part_of(part, _, b=b):
            half_gram(b, REFS, part, mine[b * 8:b * 8 + 8].reshape(2 * SEGS, 2 * BLK))
            return 0

        lax.fori_loop(0, 2, part_of, 0)
        out_copy(b, REFS).start()

    def far_copy(b, side, n):
        if side == 0:
            la, lb = TO_RIGHT[n]
            slot, a = la, lb
        else:
            la, lb = TO_LEFT[n]
            slot, a = 10 + lb, la
        return pltpu.make_async_copy(
            grecv.at[b, side, n], g_hbm.at[slot, b, a], far_sem.at[b, side, n])

    for b in range(BINS):
        for side in range(2):
            for n in range(3):
                gram_copy(b, side, n).wait_recv()
                far_copy(b, side, n).start()

    for b in range(BINS):
        for side in range(2):
            for n in range(3):
                gram_copy(b, side, n).wait_send()
                far_copy(b, side, n).wait()
        for group in range(5):
            out_copy(b, group).wait()
    for c in x_copies:
        c.wait_send()
    for side in range(2):
        inv_copy(side).wait_send()

    def drain(s, _):
        for k in range(2):
            ag_copy(0, s, k).wait_send()

            @pl.when(s < 7)
            def _():
                ag_copy(1, s, k).wait_send()
        return 0

    lax.fori_loop(0, 8, drain, 0)


def select_kernel(pairs_ref, g_hbm, pair_out, ref_out, pair_buf, ref_buf, pair_sem, ref_sem):
    base = lax.axis_index("fibre") * NBLK
    copies = []
    for a in range(NBLK):
        for p in range(NP):
            e = pairs_ref[a, p] - base + NBLK
            slot = jnp.where(e >= 10, e + 2, e)
            copies.append((
                pltpu.make_async_copy(g_hbm.at[slot, :, a], pair_buf.at[a, p], pair_sem.at[0, a, p]),
                pltpu.make_async_copy(pair_buf.at[a, p], pair_out.at[:, a, p], pair_sem.at[1, a, p])))
    for r in range(2):
        copies.append((
            pltpu.make_async_copy(g_hbm.at[10 + r], ref_buf.at[r], ref_sem.at[0, r]),
            pltpu.make_async_copy(ref_buf.at[r], ref_out.at[:, :, r], ref_sem.at[1, r])))
    for c, _ in copies:
        c.start()
    for c, d in copies:
        c.wait()
        d.start()
    for _, d in copies:
        d.wait()


def body(spectra, pairs, refs):
    bf = jnp.bfloat16
    smem = pl.BlockSpec(memory_space=pltpu.SMEM)
    hbm = pl.BlockSpec(memory_space=pl.ANY)
    dma = pltpu.SemaphoreType.DMA
    grams = pl.pallas_call(
        kernel,
        out_shape=jax.ShapeDtypeStruct((SLOTS, BINS, NBLK, 2, BLK, BLK), bf),
        in_specs=[smem, hbm],
        out_specs=hbm,
        scratch_shapes=[
            pltpu.VMEM((2, BINS, 2, SEGS, PAIR), bf),
            pltpu.VMEM((2, BINS, 2, SEGS, PAIR), bf),
            pltpu.VMEM((BINS, 2, CHAN, 2 * SEGS), bf),
            pltpu.VMEM((2, BINS, 2, SEGS, 2 * BLK), bf),
            pltpu.VMEM((NZ, 128, 2 * BLK), bf),
            pltpu.VMEM((2, 9, 128, 2 * BLK), bf),
            pltpu.VMEM((144, 2 * BLK), bf),
            pltpu.VMEM((3, 144, 2 * BLK), bf),
            pltpu.VMEM((NZ, 144, 2 * BLK), bf),
            pltpu.VMEM((BINS, 5, 2, NBLK, 2, BLK, BLK), bf),
            pltpu.VMEM((BINS, 2, 3, 2, BLK, BLK), bf),
            pltpu.VMEM((BINS, 2, 3, 2, BLK, BLK), bf),
            pltpu.VMEM((BINS, 8, CHAN), jnp.float32),
            pltpu.VMEM((2, 8, CHAN), jnp.float32),
            pltpu.VMEM((BINS, 8, CHAN), jnp.float32),
            pltpu.VMEM((2, BINS, 8, 2 * BLK), jnp.float32),
            pltpu.VMEM((2, 16, CHAN), bf),
            dma((BINS, 2)),
            dma((2,)), dma((2,)),
            dma((2, 12)), dma((2, 12)),
            dma((2, 8, 2)), dma((2, 8, 2)),
            dma((3,)), dma((3,)),
            dma((2, 8, 2)), dma((2, 8, 2)),
            dma((BINS, 2, 3)), dma((BINS, 2, 3)),
            dma((2,)), dma((2,)),
            dma((BINS, 5)),
            dma((BINS, 2, 3)),
        ],
        compiler_params=pltpu.CompilerParams(
            collective_id=0, has_side_effects=True, vmem_limit_bytes=60 * 1024 * 1024),
        cost_estimate=pl.CostEstimate(
            flops=5_400_000_000, bytes_accessed=8 * 1024 * 1024, transcendentals=1024),
        name="grams",
    )(refs, spectra)
    return pl.pallas_call(
        select_kernel,
        out_shape=(
            jax.ShapeDtypeStruct((BINS, NBLK, NP, 2, BLK, BLK), bf),
            jax.ShapeDtypeStruct((BINS, NBLK, 2, 2, BLK, BLK), bf),
        ),
        in_specs=[smem, hbm],
        out_specs=(hbm, hbm),
        scratch_shapes=[
            pltpu.VMEM((NBLK, NP, BINS, 2, BLK, BLK), bf),
            pltpu.VMEM((2, BINS, NBLK, 2, BLK, BLK), bf),
            dma((2, NBLK, NP)), dma((2, 2)),
        ],
        compiler_params=pltpu.CompilerParams(vmem_limit_bytes=60 * 1024 * 1024),
        cost_estimate=pl.CostEstimate(
            flops=0, bytes_accessed=6 * 1024 * 1024, transcendentals=0),
        name="select",
    )(pairs, grams)


def solution(mesh):
    return jax.shard_map(
        body,
        mesh=mesh,
        in_specs=(P("freq", None, None, "fibre"), P("fibre", None), P()),
        out_specs=(
            P("freq", "fibre", None, None, None, None),
            P("freq", "fibre", None, None, None, None),
        ),
        check_vma=False,
    )
```

```python
import math

import jax
import jax.numpy as jnp
from jax import lax
from jax.experimental import pallas as pl
from jax.experimental.pallas import tpu as pltpu
from jax.sharding import PartitionSpec as P

BLK = 128
NP = 4
SEGS = 512
EPS = 1e-06
BINS = 2
NBLK = 4
CHAN = NBLK * BLK
PAIR = 2 * BLK
NX = 4
NZ = 16
NF = 8
NFIB = NX * NZ
SCALE = 1.0 / math.sqrt(SEGS)
MESH = pl.DeviceIdType.MESH
TO_RIGHT = ((0, 0), (1, 0), (1, 1))
TO_LEFT = ((2, 2), (3, 2), (3, 3))
SLOTS = 14
LEFT, OWN0, OWN1, RIGHT, REFS = range(5)
PIECES = (
    (0, 0, 0, 128), (0, 0, 128, 256), (0, 0, 384, 128),
    (0, 1, 0, 256), (0, 1, 256, 128), (0, 1, 384, 128),
    (1, 0, 0, 256), (1, 0, 256, 128), (1, 0, 384, 128),
    (1, 1, 0, 128), (1, 1, 128, 128), (1, 1, 256, 256),
)


def kernel(
    refs_ref, spec_hbm, g_hbm,
    raw, white, lhs, halo, mine, ring, xsend, xrecv, full, stage, gsend, grecv,
    psend, precv, inv_own, inv_halo, mask_ref, wref,
    load_sem, pow_s, pow_r, halo_s, halo_r, ring_s, ring_r, x_s, x_r, ag_s, ag_r,
    gs_s, gs_r, inv_s, inv_r, out_sem, far_sem,
):
    f32, bf = jnp.float32, jnp.bfloat16
    fq = lax.axis_index("freq")
    fb = lax.axis_index("fibre")
    x = lax.rem(fb, NX)
    z = fb // NX
    f_up, f_dn = lax.rem(fq + 1, NF), lax.rem(fq + NF - 1, NF)
    right, left = lax.rem(fb + 1, NFIB), lax.rem(fb + NFIB - 1, NFIB)
    z_up, z_dn = lax.rem(fb + NX, NFIB), lax.rem(fb + NFIB - NX, NFIB)
    peers = [z * NX + lax.rem(x + o, NX) for o in (1, 2, 3)]

    def remote(src, dst, s_sem, r_sem, f, d):
        return pltpu.make_async_remote_copy(
            src, dst, s_sem, r_sem, device_id=(f, d), device_id_type=MESH)

    loads = [
        pltpu.make_async_copy(
            spec_hbm.at[b, :, :, pl.ds(h * PAIR, PAIR)], raw.at[h, b], load_sem.at[b, h])
        for b in range(BINS) for h in range(2)
    ]
    for c in loads:
        c.start()

    barrier = pltpu.get_barrier_semaphore()
    for f in (f_up, f_dn):
        pl.semaphore_signal(barrier, inc=1, device_id=(f, fb), device_id_type=MESH)
    for d in [right, left, z_up, z_dn] + peers:
        pl.semaphore_signal(barrier, inc=1, device_id=(fq, d), device_id_type=MESH)

    block = fb * NBLK + lax.broadcasted_iota(jnp.int32, (16, CHAN), 1) // BLK
    for r in range(2):
        mask_ref[r] = jnp.where(block == refs_ref[r], 1.0, 0.0).astype(bf)

    def gather_lanes(t):
        return (t[..., :BLK] + t[..., BLK:2 * BLK]) + (t[..., 2 * BLK:3 * BLK] + t[..., 3 * BLK:])

    def gather_two(t):
        return t[..., :BLK] + t[..., BLK:]

    for b in range(BINS):
        loads[2 * b].wait()
        loads[2 * b + 1].wait()

        def pick(i, _, b=b):
            for part in range(2):
                v = [raw[h, b, part, pl.ds(i * 128, 128), :].reshape(8, 16, PAIR) for h in range(2)]
                for r in range(2):
                    m = mask_ref[r]
                    t = gather_two(v[0] * m[None, :, :PAIR]) + gather_two(v[1] * m[None, :, PAIR:])
                    mine[b * 8 + part * 4 + i, :, r * BLK:(r + 1) * BLK] = t.reshape(128, BLK)
            return 0

        lax.fori_loop(0, 4, pick, 0)

    def ring_copy(way, s, k):
        rows = pl.ds(k * 64, 64)
        src = mine.at[lax.rem(z + 8, NZ) if way == 0 else lax.rem(z + NZ - 7, NZ), rows]
        if not (isinstance(s, int) and s == 0):
            src = ring.at[way, s, rows]
        return remote(src, ring.at[way, s + 1, rows], ring_s.at[way, s, k], ring_r.at[way, s, k],
                      fq, z_up if way == 0 else z_dn)

    def halo_copy(n, side):
        b, part, first, size = PIECES[n]
        rows = pl.ds(first, size)
        return remote(raw.at[1 - side, b, part, rows], halo.at[side, b, part, rows],
                      halo_s.at[side, n], halo_r.at[side, n], fq, right if side == 0 else left)

    def inv_copy(side):
        cols = pl.ds(2 * BLK, 2 * BLK) if side == 0 else pl.ds(0, 2 * BLK)
        return remote(inv_own.at[:, :, cols], inv_halo.at[side], inv_s.at[side], inv_r.at[side],
                      fq, right if side == 0 else left)

    pl.semaphore_wait(barrier, 9)
    for k in range(2):
        for way in range(2):
            ring_copy(way, 0, k).start()

    def halo_start(piece):
        for side in range(2):
            halo_copy(piece, side).start()

    halo_start(0)

    def reduce_step(s):
        for k in range(2):
            rows = pl.ds(k * 64, 64)
            ring_copy(0, s, k).wait_recv()
            ring[0, s + 1, rows] = ring[0, s + 1, rows] + mine[lax.rem(z + 7 - s + NZ, NZ), rows]
            if s < 7:
                ring_copy(0, s + 1, k).start()
            if s < 7:
                ring_copy(1, s, k).wait_recv()
            if s < 6:
                ring[1, s + 1, rows] = ring[1, s + 1, rows] + mine[lax.rem(z + NZ - 6 + s, NZ), rows]
                ring_copy(1, s + 1, k).start()

    for b in range(BINS):
        def add(i, acc, b=b):
            for part in range(2):
                v = [raw[h, b, part, pl.ds(i * 64, 64), :].astype(f32) for h in range(2)]
                acc = [a + jnp.sum((w * w).reshape(8, 8, PAIR), axis=0) for a, w in zip(acc, v)]
            return acc

        acc = lax.fori_loop(0, SEGS // 64, add, [jnp.zeros((8, PAIR), f32)] * 2)
        psend[b, :, :PAIR] = acc[0]
        psend[b, :, PAIR:] = acc[1]

    up = remote(psend.at[1], precv.at[0], pow_s.at[0], pow_r.at[0], f_up, fb)
    dn = remote(psend.at[0], precv.at[1], pow_s.at[1], pow_r.at[1], f_dn, fb)
    up.start()
    dn.start()
    reduce_step(0)
    halo_start(1)

    def total(v):
        return jnp.sum(v, axis=0, keepdims=True) / SEGS

    p0, p1 = total(psend[0]), total(psend[1])
    up.wait()
    dn.wait()
    below = jnp.where(fq == 0, 0.0, total(precv[0]))
    above = jnp.where(fq == NF - 1, 0.0, total(precv[1]))
    c0 = jnp.where(fq == 0, 2.0, 3.0)
    c1 = jnp.where(fq == NF - 1, 2.0, 3.0)
    smooth = [(below + p0 + p1) / c0, (p0 + p1 + above) / c1]
    row = lax.broadcasted_iota(jnp.int32, (16, BLK), 0)
    for b in range(BINS):
        inv_own[b] = jnp.broadcast_to(1.0 / jnp.sqrt(smooth[b] + EPS), (8, CHAN))
    inv_copy(0).start()
    inv_copy(1).start()
    for r in range(2):
        tile = jnp.zeros((16, BLK), f32)
        for b in range(BINS):
            v = gather_lanes(inv_own[b, 0:1, :] * mask_ref[r, 0:1, :].astype(f32))
            for piece in range(3):
                part = v.astype(bf).astype(f32)
                tile = jnp.where(row == b * 3 + piece, jnp.broadcast_to(part, (16, BLK)), tile)
                v = v - part
        xsend[128:144, r * BLK:(r + 1) * BLK] = tile.astype(bf)
    reduce_step(1)
    halo_start(2)

    def whiten(b):
        def turn(i, _):
            rows = pl.ds(pl.multiple_of(i * 128, 128), 128)
            rows2 = pl.ds(pl.multiple_of(SEGS + i * 128, 128), 128)
            for h in range(2):
                cols = slice(h * PAIR, (h + 1) * PAIR)
                inv = inv_own[b, 0:1, cols]
                re = (raw[h, b, 0, rows, :].astype(f32) * inv).astype(bf)
                im = (raw[h, b, 1, rows, :].astype(f32) * inv).astype(bf)
                white[h, b, 0, rows, :] = re
                white[h, b, 1, rows, :] = im
                re, im = re.T, im.T
                lhs[b, 0, cols, rows] = re
                lhs[b, 0, cols, rows2] = im
                lhs[b, 1, cols, rows] = -im
                lhs[b, 1, cols, rows2] = re
            return 0

        lax.fori_loop(0, SEGS // 128, turn, 0)

    def half_gram(b, group, part, rhs):
        res = jnp.dot(lhs[b, part], rhs, preferred_element_type=f32) * SCALE
        res = res.astype(bf)
        for q in range(2):
            for a in range(NBLK):
                stage[b, group, q, a, part] = res[a * BLK:(a + 1) * BLK, q * BLK:(q + 1) * BLK]

    def out_copy(b, group):
        return pltpu.make_async_copy(
            stage.at[b, group], g_hbm.at[pl.ds(2 + 2 * group, 2), b], out_sem.at[b, group])

    def own_grams(b, pair):
        def part_of(part, _):
            half_gram(b, OWN0 + pair, part, white[pair, b].reshape(2 * SEGS, 2 * BLK))
            return 0

        lax.fori_loop(0, 2, part_of, 0)
        out_copy(b, OWN0 + pair).start()

    whiten(0)
    reduce_step(2)
    halo_start(3)
    whiten(1)
    reduce_step(3)
    halo_start(4)
    own_grams(0, 0)
    reduce_step(4)
    halo_start(5)
    own_grams(0, 1)
    reduce_step(5)
    halo_start(6)
    own_grams(1, 0)
    reduce_step(6)
    halo_start(7)
    own_grams(1, 1)
    for k in range(2):
        ring_copy(0, 7, k).wait_recv()
    xsend[0:128] = mine[z] + ring[0, 8] + ring[1, 7]

    x_copies = [
        remote(xsend, xrecv.at[o], x_s.at[o], x_r.at[o], fq, peers[o]) for o in range(3)
    ]
    for c in x_copies:
        c.start()

    def gram_copy(b, side, n):
        return remote(gsend.at[b, side, n], grecv.at[b, side, n], gs_s.at[b, side, n],
                      gs_r.at[b, side, n], fq, right if side == 0 else left)

    def halo_grams(b, side):
        group = RIGHT if side else LEFT
        for n in range(b * 6, b * 6 + 6):
            halo_copy(n, side).wait_recv()

        def scale(i, _):
            rows = pl.ds(i * 64, 64)
            for part in range(2):
                v = halo[side, b, part, rows, :].astype(f32) * inv_halo[side, b, 0:1, :]
                halo[side, b, part, rows, :] = v.astype(bf)
            return 0

        lax.fori_loop(0, SEGS // 64, scale, 0)

        def part_of(part, _):
            half_gram(b, group, part, halo[side, b].reshape(2 * SEGS, 2 * BLK))
            return 0

        lax.fori_loop(0, 2, part_of, 0)
        out_copy(b, group).start()
        if side == 1:
            for n, (la, lb) in enumerate(TO_RIGHT):
                gsend[b, 0, n, 0] = stage[b, RIGHT, lb, la, 0].T
                gsend[b, 0, n, 1] = -stage[b, RIGHT, lb, la, 1].T
        else:
            for n, (la, lb) in enumerate(TO_LEFT):
                gsend[b, 1, n, 0] = stage[b, LEFT, la - 2, lb, 0].T
                gsend[b, 1, n, 1] = -stage[b, LEFT, la - 2, lb, 1].T

    inv_copy(0).wait_recv()
    inv_copy(1).wait_recv()
    halo_grams(0, 0)
    for s in range(8):
        for k in range(2):
            ring_copy(0, s, k).wait_send()
            if s < 7:
                ring_copy(1, s, k).wait_send()

    for c in x_copies:
        c.wait_recv()
    full[z] = xsend[...] + xrecv[0] + xrecv[1] + xrecv[2]

    def ag_copy(way, s, k):
        rows = pl.ds(0, 64) if k == 0 else pl.ds(64, 80)
        c = lax.rem(z + NZ - s, NZ) if way == 0 else lax.rem(z + s, NZ)
        return remote(full.at[c, rows], full.at[c, rows], ag_s.at[way, s, k], ag_r.at[way, s, k],
                      fq, z_up if way == 0 else z_dn)

    for k in range(2):
        for way in range(2):
            ag_copy(way, 0, k).start()

    def gather_step(s):
        for k in range(2):
            ag_copy(0, s, k).wait_recv()
            if s < 7:
                ag_copy(0, s + 1, k).start()
                ag_copy(1, s, k).wait_recv()
            if s < 6:
                ag_copy(1, s + 1, k).start()
        if s > 0:
            for k in range(2):
                ag_copy(0, s - 1, k).wait_send()
                ag_copy(1, s - 1, k).wait_send()

    def far_copy(b, side, n):
        if side == 0:
            la, lb = TO_RIGHT[n]
            slot, a = la, lb
        else:
            la, lb = TO_LEFT[n]
            slot, a = 10 + lb, la
        return pltpu.make_async_copy(
            grecv.at[b, side, n], g_hbm.at[slot, b, a], far_sem.at[b, side, n])

    def far_start(b):
        for side in range(2):
            for n in range(3):
                gram_copy(b, side, n).wait_recv()
                far_copy(b, side, n).start()

    gather_step(0)
    halo_start(8)
    halo_grams(0, 1)
    gather_step(1)
    halo_start(9)
    for s in range(2, 4):
        gather_step(s)
        halo_start(8 + s)
        for side in range(2):
            gram_copy(0, side, s - 2).start()
    gather_step(4)
    for side in range(2):
        gram_copy(0, side, 2).start()
    halo_grams(1, 0)
    gather_step(5)
    gram_copy(1, 1, 0).start()
    gram_copy(1, 1, 1).start()
    halo_grams(1, 1)
    gather_step(6)
    gram_copy(1, 1, 2).start()
    gram_copy(1, 0, 0).start()
    far_start(0)
    gather_step(7)
    gram_copy(1, 0, 1).start()
    gram_copy(1, 0, 2).start()

    tail = full[0, 128:144, :].astype(f32)
    for c in range(1, NZ):
        tail = tail + full[c, 128:144, :].astype(f32)
    for b in range(BINS):
        inv = tail[b * 3:b * 3 + 1] + tail[b * 3 + 1:b * 3 + 2] + tail[b * 3 + 2:b * 3 + 3]

        def scale(i, _, b=b, inv=inv):
            c = b * 8 + i // 2
            rows = pl.ds(pl.multiple_of(lax.rem(i, 2) * 64, 64), 64)
            wref[c, rows, :] = (full[c, rows, :].astype(f32) * inv).astype(bf)
            return 0

        lax.fori_loop(0, 16, scale, 0)

        def part_of(part, _, b=b):
            half_gram(b, REFS, part, wref[b * 8:b * 8 + 8].reshape(2 * SEGS, 2 * BLK))
            return 0

        lax.fori_loop(0, 2, part_of, 0)
        out_copy(b, REFS).start()

    far_start(1)
    for n in range(12):
        for side in range(2):
            halo_copy(n, side).wait_send()
    for c in x_copies:
        c.wait_send()
    for side in range(2):
        inv_copy(side).wait_send()
    for k in range(2):
        ag_copy(0, 7, k).wait_send()
    for b in range(BINS):
        for side in range(2):
            for n in range(3):
                gram_copy(b, side, n).wait_send()
                far_copy(b, side, n).wait()
        for group in range(5):
            out_copy(b, group).wait()


def select_kernel(pairs_ref, g_hbm, pair_out, ref_out, pair_buf, ref_buf, pair_sem, ref_sem):
    base = lax.axis_index("fibre") * NBLK
    copies = []
    for a in range(NBLK):
        for p in range(NP):
            e = pairs_ref[a, p] - base + NBLK
            slot = jnp.where(e >= 10, e + 2, e)
            copies.append((
                pltpu.make_async_copy(g_hbm.at[slot, :, a], pair_buf.at[a, p], pair_sem.at[0, a, p]),
                pltpu.make_async_copy(pair_buf.at[a, p], pair_out.at[:, a, p], pair_sem.at[1, a, p])))
    for r in range(2):
        copies.append((
            pltpu.make_async_copy(g_hbm.at[10 + r], ref_buf.at[r], ref_sem.at[0, r]),
            pltpu.make_async_copy(ref_buf.at[r], ref_out.at[:, :, r], ref_sem.at[1, r])))
    for c, _ in copies:
        c.start()
    for c, d in copies:
        c.wait()
        d.start()
    for _, d in copies:
        d.wait()


def body(spectra, pairs, refs):
    bf = jnp.bfloat16
    smem = pl.BlockSpec(memory_space=pltpu.SMEM)
    hbm = pl.BlockSpec(memory_space=pl.ANY)
    dma = pltpu.SemaphoreType.DMA
    grams = pl.pallas_call(
        kernel,
        out_shape=jax.ShapeDtypeStruct((SLOTS, BINS, NBLK, 2, BLK, BLK), bf),
        in_specs=[smem, hbm],
        out_specs=hbm,
        scratch_shapes=[
            pltpu.VMEM((2, BINS, 2, SEGS, PAIR), bf),
            pltpu.VMEM((2, BINS, 2, SEGS, PAIR), bf),
            pltpu.VMEM((BINS, 2, CHAN, 2 * SEGS), bf),
            pltpu.VMEM((2, BINS, 2, SEGS, 2 * BLK), bf),
            pltpu.VMEM((NZ, 128, 2 * BLK), bf),
            pltpu.VMEM((2, 9, 128, 2 * BLK), bf),
            pltpu.VMEM((144, 2 * BLK), bf),
            pltpu.VMEM((3, 144, 2 * BLK), bf),
            pltpu.VMEM((NZ, 144, 2 * BLK), bf),
            pltpu.VMEM((BINS, 5, 2, NBLK, 2, BLK, BLK), bf),
            pltpu.VMEM((BINS, 2, 3, 2, BLK, BLK), bf),
            pltpu.VMEM((BINS, 2, 3, 2, BLK, BLK), bf),
            pltpu.VMEM((BINS, 8, CHAN), jnp.float32),
            pltpu.VMEM((2, 8, CHAN), jnp.float32),
            pltpu.VMEM((BINS, 8, CHAN), jnp.float32),
            pltpu.VMEM((2, BINS, 8, 2 * BLK), jnp.float32),
            pltpu.VMEM((2, 16, CHAN), bf),
            pltpu.VMEM((NZ, 128, 2 * BLK), bf),
            dma((BINS, 2)),
            dma((2,)), dma((2,)),
            dma((2, 12)), dma((2, 12)),
            dma((2, 8, 2)), dma((2, 8, 2)),
            dma((3,)), dma((3,)),
            dma((2, 8, 2)), dma((2, 8, 2)),
            dma((BINS, 2, 3)), dma((BINS, 2, 3)),
            dma((2,)), dma((2,)),
            dma((BINS, 5)),
            dma((BINS, 2, 3)),
        ],
        compiler_params=pltpu.CompilerParams(
            collective_id=0, has_side_effects=True, vmem_limit_bytes=60 * 1024 * 1024),
        cost_estimate=pl.CostEstimate(
            flops=5_400_000_000, bytes_accessed=8 * 1024 * 1024, transcendentals=1024),
        name="grams",
    )(refs, spectra)
    return pl.pallas_call(
        select_kernel,
        out_shape=(
            jax.ShapeDtypeStruct((BINS, NBLK, NP, 2, BLK, BLK), bf),
            jax.ShapeDtypeStruct((BINS, NBLK, 2, 2, BLK, BLK), bf),
        ),
        in_specs=[smem, hbm],
        out_specs=(hbm, hbm),
        scratch_shapes=[
            pltpu.VMEM((NBLK, NP, BINS, 2, BLK, BLK), bf),
            pltpu.VMEM((2, BINS, NBLK, 2, BLK, BLK), bf),
            dma((2, NBLK, NP)), dma((2, 2)),
        ],
        compiler_params=pltpu.CompilerParams(vmem_limit_bytes=60 * 1024 * 1024),
        cost_estimate=pl.CostEstimate(
            flops=0, bytes_accessed=6 * 1024 * 1024, transcendentals=0),
        name="select",
    )(pairs, grams)


def solution(mesh):
    return jax.shard_map(
        body,
        mesh=mesh,
        in_specs=(P("freq", None, None, "fibre"), P("fibre", None), P()),
        out_specs=(
            P("freq", "fibre", None, None, None, None),
            P("freq", "fibre", None, None, None, None),
        ),
        check_vma=False,
    )
```

```python
import math

import jax
import jax.numpy as jnp
from jax import lax
from jax.experimental import pallas as pl
from jax.experimental.pallas import tpu as pltpu
from jax.sharding import PartitionSpec as P

BLK = 128
NP = 4
SEGS = 512
EPS = 1e-06
BINS = 2
NBLK = 4
CHAN = NBLK * BLK
PAIR = 2 * BLK
NX = 4
NZ = 16
NF = 8
NFIB = NX * NZ
SCALE = 1.0 / math.sqrt(SEGS)
MESH = pl.DeviceIdType.MESH
TO_RIGHT = ((0, 0), (1, 0), (1, 1))
TO_LEFT = ((2, 2), (3, 2), (3, 3))
SLOTS = 14
LEFT, OWN0, OWN1, RIGHT, REFS = range(5)
PIECES = (
    (0, 0, 0, 128), (0, 0, 128, 256), (0, 0, 384, 128),
    (0, 1, 0, 256), (0, 1, 256, 128), (0, 1, 384, 128),
    (1, 0, 0, 256), (1, 0, 256, 128), (1, 0, 384, 128),
    (1, 1, 0, 128), (1, 1, 128, 128), (1, 1, 256, 256),
)


def kernel(
    refs_ref, spec_hbm, g_hbm,
    raw, white, lhs, halo, mine, ring, xsend, xrecv, full, stage, gsend, grecv,
    psend, precv, inv_own, inv_halo, mask_ref, wref,
    load_sem, pow_s, pow_r, halo_s, halo_r, ring_s, ring_r, x_s, x_r, ag_s, ag_r,
    gs_s, gs_r, inv_s, inv_r, out_sem, far_sem,
):
    f32, bf = jnp.float32, jnp.bfloat16
    fq = lax.axis_index("freq")
    fb = lax.axis_index("fibre")
    x = lax.rem(fb, NX)
    z = fb // NX
    f_up, f_dn = lax.rem(fq + 1, NF), lax.rem(fq + NF - 1, NF)
    right, left = lax.rem(fb + 1, NFIB), lax.rem(fb + NFIB - 1, NFIB)
    z_up, z_dn = lax.rem(fb + NX, NFIB), lax.rem(fb + NFIB - NX, NFIB)
    peers = [z * NX + lax.rem(x + o, NX) for o in (1, 2, 3)]

    def remote(src, dst, s_sem, r_sem, f, d):
        return pltpu.make_async_remote_copy(
            src, dst, s_sem, r_sem, device_id=(f, d), device_id_type=MESH)

    loads = [
        pltpu.make_async_copy(
            spec_hbm.at[b, :, :, pl.ds(h * PAIR, PAIR)], raw.at[h, b], load_sem.at[b, h])
        for b in range(BINS) for h in range(2)
    ]
    for c in loads:
        c.start()

    barrier = pltpu.get_barrier_semaphore()
    for f in (f_up, f_dn):
        pl.semaphore_signal(barrier, inc=1, device_id=(f, fb), device_id_type=MESH)
    for d in [right, left, z_up, z_dn] + peers:
        pl.semaphore_signal(barrier, inc=1, device_id=(fq, d), device_id_type=MESH)

    block = fb * NBLK + lax.broadcasted_iota(jnp.int32, (16, CHAN), 1) // BLK
    for r in range(2):
        mask_ref[r] = jnp.where(block == refs_ref[r], 1.0, 0.0).astype(bf)

    def gather_lanes(t):
        return (t[..., :BLK] + t[..., BLK:2 * BLK]) + (t[..., 2 * BLK:3 * BLK] + t[..., 3 * BLK:])

    def gather_two(t):
        return t[..., :BLK] + t[..., BLK:]

    for b in range(BINS):
        loads[2 * b].wait()
        loads[2 * b + 1].wait()

        def pick(i, _, b=b):
            for part in range(2):
                v = [raw[h, b, part, pl.ds(i * 128, 128), :].reshape(8, 16, PAIR) for h in range(2)]
                for r in range(2):
                    m = mask_ref[r]
                    t = gather_two(v[0] * m[None, :, :PAIR]) + gather_two(v[1] * m[None, :, PAIR:])
                    mine[b * 8 + part * 4 + i, :, r * BLK:(r + 1) * BLK] = t.reshape(128, BLK)
            return 0

        lax.fori_loop(0, 4, pick, 0)

    def ring_copy(way, s, k):
        rows = pl.ds(k * 64, 64)
        src = mine.at[lax.rem(z + 8, NZ) if way == 0 else lax.rem(z + NZ - 7, NZ), rows]
        if not (isinstance(s, int) and s == 0):
            src = ring.at[way, s, rows]
        return remote(src, ring.at[way, s + 1, rows], ring_s.at[way, s, k], ring_r.at[way, s, k],
                      fq, z_up if way == 0 else z_dn)

    def halo_copy(n, side):
        b, part, first, size = PIECES[n]
        rows = pl.ds(first, size)
        return remote(raw.at[1 - side, b, part, rows], halo.at[side, b, part, rows],
                      halo_s.at[side, n], halo_r.at[side, n], fq, right if side == 0 else left)

    def inv_copy(side):
        cols = pl.ds(2 * BLK, 2 * BLK) if side == 0 else pl.ds(0, 2 * BLK)
        return remote(inv_own.at[:, :, cols], inv_halo.at[side], inv_s.at[side], inv_r.at[side],
                      fq, right if side == 0 else left)

    pl.semaphore_wait(barrier, 9)
    for k in range(2):
        for way in range(2):
            ring_copy(way, 0, k).start()

    def halo_start(piece):
        for side in range(2):
            halo_copy(piece, side).start()

    halo_start(0)

    def reduce_step(s):
        for k in range(2):
            rows = pl.ds(k * 64, 64)
            ring_copy(0, s, k).wait_recv()
            ring[0, s + 1, rows] = ring[0, s + 1, rows] + mine[lax.rem(z + 7 - s + NZ, NZ), rows]
            if s < 7:
                ring_copy(0, s + 1, k).start()
            if s < 7:
                ring_copy(1, s, k).wait_recv()
            if s < 6:
                ring[1, s + 1, rows] = ring[1, s + 1, rows] + mine[lax.rem(z + NZ - 6 + s, NZ), rows]
                ring_copy(1, s + 1, k).start()

    for b in range(BINS):
        def add(i, acc, b=b):
            for part in range(2):
                v = [raw[h, b, part, pl.ds(i * 64, 64), :].astype(f32) for h in range(2)]
                acc = [a + jnp.sum((w * w).reshape(8, 8, PAIR), axis=0) for a, w in zip(acc, v)]
            return acc

        acc = lax.fori_loop(0, SEGS // 64, add, [jnp.zeros((8, PAIR), f32)] * 2)
        psend[b, :, :PAIR] = acc[0]
        psend[b, :, PAIR:] = acc[1]

    up = remote(psend.at[1], precv.at[0], pow_s.at[0], pow_r.at[0], f_up, fb)
    dn = remote(psend.at[0], precv.at[1], pow_s.at[1], pow_r.at[1], f_dn, fb)
    up.start()
    dn.start()
    reduce_step(0)
    halo_start(1)

    def total(v):
        return jnp.sum(v, axis=0, keepdims=True) / SEGS

    p0, p1 = total(psend[0]), total(psend[1])
    up.wait()
    dn.wait()
    below = jnp.where(fq == 0, 0.0, total(precv[0]))
    above = jnp.where(fq == NF - 1, 0.0, total(precv[1]))
    c0 = jnp.where(fq == 0, 2.0, 3.0)
    c1 = jnp.where(fq == NF - 1, 2.0, 3.0)
    smooth = [(below + p0 + p1) / c0, (p0 + p1 + above) / c1]
    row = lax.broadcasted_iota(jnp.int32, (16, BLK), 0)
    for b in range(BINS):
        inv_own[b] = jnp.broadcast_to(1.0 / jnp.sqrt(smooth[b] + EPS), (8, CHAN))
    inv_copy(0).start()
    inv_copy(1).start()
    for r in range(2):
        tile = jnp.zeros((16, BLK), f32)
        for b in range(BINS):
            v = gather_lanes(inv_own[b, 0:1, :] * mask_ref[r, 0:1, :].astype(f32))
            for piece in range(3):
                part = v.astype(bf).astype(f32)
                tile = jnp.where(row == b * 3 + piece, jnp.broadcast_to(part, (16, BLK)), tile)
                v = v - part
        xsend[128:144, r * BLK:(r + 1) * BLK] = tile.astype(bf)
    reduce_step(1)
    halo_start(2)

    def whiten(b):
        def turn(i, _):
            rows = pl.ds(pl.multiple_of(i * 128, 128), 128)
            rows2 = pl.ds(pl.multiple_of(SEGS + i * 128, 128), 128)
            for h in range(2):
                cols = slice(h * PAIR, (h + 1) * PAIR)
                inv = inv_own[b, 0:1, cols]
                re = (raw[h, b, 0, rows, :].astype(f32) * inv).astype(bf)
                im = (raw[h, b, 1, rows, :].astype(f32) * inv).astype(bf)
                white[h, b, 0, rows, :] = re
                white[h, b, 1, rows, :] = im
                re, im = re.T, im.T
                lhs[b, 0, cols, rows] = re
                lhs[b, 0, cols, rows2] = im
                lhs[b, 1, cols, rows] = -im
                lhs[b, 1, cols, rows2] = re
            return 0

        lax.fori_loop(0, SEGS // 128, turn, 0)

    def half_gram(b, group, part, rhs):
        res = jnp.dot(lhs[b, part], rhs, preferred_element_type=f32) * SCALE
        res = res.astype(bf)
        for q in range(2):
            for a in range(NBLK):
                stage[b, group, q, a, part] = res[a * BLK:(a + 1) * BLK, q * BLK:(q + 1) * BLK]

    def out_copy(b, group):
        return pltpu.make_async_copy(
            stage.at[b, group], g_hbm.at[pl.ds(2 + 2 * group, 2), b], out_sem.at[b, group])

    def own_grams(b, pair):
        def part_of(part, _):
            half_gram(b, OWN0 + pair, part, white[pair, b].reshape(2 * SEGS, 2 * BLK))
            return 0

        lax.fori_loop(0, 2, part_of, 0)
        out_copy(b, OWN0 + pair).start()

    whiten(0)
    reduce_step(2)
    halo_start(3)
    whiten(1)
    reduce_step(3)
    halo_start(4)
    own_grams(0, 0)
    reduce_step(4)
    halo_start(5)
    own_grams(0, 1)
    reduce_step(5)
    halo_start(6)
    own_grams(1, 0)
    reduce_step(6)
    halo_start(7)
    own_grams(1, 1)
    for k in range(2):
        ring_copy(0, 7, k).wait_recv()
    xsend[0:128] = mine[z] + ring[0, 8] + ring[1, 7]

    x_copies = [
        remote(xsend, xrecv.at[o], x_s.at[o], x_r.at[o], fq, peers[o]) for o in range(3)
    ]
    for c in x_copies:
        c.start()

    def gram_copy(b, side, n):
        return remote(gsend.at[b, side, n], grecv.at[b, side, n], gs_s.at[b, side, n],
                      gs_r.at[b, side, n], fq, right if side == 0 else left)

    def halo_grams(b, side):
        group = RIGHT if side else LEFT
        for n in range(b * 6, b * 6 + 6):
            halo_copy(n, side).wait_recv()

        def scale(i, _):
            rows = pl.ds(i * 64, 64)
            for part in range(2):
                v = halo[side, b, part, rows, :].astype(f32) * inv_halo[side, b, 0:1, :]
                halo[side, b, part, rows, :] = v.astype(bf)
            return 0

        lax.fori_loop(0, SEGS // 64, scale, 0)

        def part_of(part, _):
            half_gram(b, group, part, halo[side, b].reshape(2 * SEGS, 2 * BLK))
            return 0

        lax.fori_loop(0, 2, part_of, 0)
        out_copy(b, group).start()
        if side == 1:
            for n, (la, lb) in enumerate(TO_RIGHT):
                gsend[b, 0, n, 0] = stage[b, RIGHT, lb, la, 0].T
                gsend[b, 0, n, 1] = -stage[b, RIGHT, lb, la, 1].T
        else:
            for n, (la, lb) in enumerate(TO_LEFT):
                gsend[b, 1, n, 0] = stage[b, LEFT, la - 2, lb, 0].T
                gsend[b, 1, n, 1] = -stage[b, LEFT, la - 2, lb, 1].T

    inv_copy(0).wait_recv()
    inv_copy(1).wait_recv()
    halo_grams(0, 0)
    for s in range(8):
        for k in range(2):
            ring_copy(0, s, k).wait_send()
            if s < 7:
                ring_copy(1, s, k).wait_send()

    for c in x_copies:
        c.wait_recv()
    full[z] = xsend[...] + xrecv[0] + xrecv[1] + xrecv[2]

    def ag_copy(way, s, k):
        c = lax.rem(z + NZ - s, NZ) if way == 0 else lax.rem(z + s, NZ)
        return remote(full.at[c], full.at[c], ag_s.at[way, s, k], ag_r.at[way, s, k],
                      fq, z_up if way == 0 else z_dn)

    for k in range(1):
        for way in range(2):
            ag_copy(way, 0, k).start()

    def gather_step(s):
        for k in range(1):
            ag_copy(0, s, k).wait_recv()
            if s < 7:
                ag_copy(0, s + 1, k).start()
                ag_copy(1, s, k).wait_recv()
            if s < 6:
                ag_copy(1, s + 1, k).start()
        if s > 0:
            for k in range(1):
                ag_copy(0, s - 1, k).wait_send()
                ag_copy(1, s - 1, k).wait_send()

    def far_copy(b, side, n):
        if side == 0:
            la, lb = TO_RIGHT[n]
            slot, a = la, lb
        else:
            la, lb = TO_LEFT[n]
            slot, a = 10 + lb, la
        return pltpu.make_async_copy(
            grecv.at[b, side, n], g_hbm.at[slot, b, a], far_sem.at[b, side, n])

    def far_start(b):
        for side in range(2):
            for n in range(3):
                gram_copy(b, side, n).wait_recv()
                far_copy(b, side, n).start()

    gather_step(0)
    halo_start(8)
    halo_grams(0, 1)
    gather_step(1)
    halo_start(9)
    for s in range(2, 4):
        gather_step(s)
        halo_start(8 + s)
        for side in range(2):
            gram_copy(0, side, s - 2).start()
    gather_step(4)
    for side in range(2):
        gram_copy(0, side, 2).start()
    halo_grams(1, 0)
    gather_step(5)
    gram_copy(1, 1, 0).start()
    gram_copy(1, 1, 1).start()
    halo_grams(1, 1)
    gather_step(6)
    gram_copy(1, 1, 2).start()
    gram_copy(1, 0, 0).start()
    far_start(0)
    gather_step(7)
    gram_copy(1, 0, 1).start()
    gram_copy(1, 0, 2).start()

    tail = full[0, 128:144, :].astype(f32)
    for c in range(1, NZ):
        tail = tail + full[c, 128:144, :].astype(f32)
    for b in range(BINS):
        inv = tail[b * 3:b * 3 + 1] + tail[b * 3 + 1:b * 3 + 2] + tail[b * 3 + 2:b * 3 + 3]

        def scale(i, _, b=b, inv=inv):
            c = b * 8 + i // 2
            rows = pl.ds(pl.multiple_of(lax.rem(i, 2) * 64, 64), 64)
            wref[c, rows, :] = (full[c, rows, :].astype(f32) * inv).astype(bf)
            return 0

        lax.fori_loop(0, 16, scale, 0)

        def part_of(part, _, b=b):
            half_gram(b, REFS, part, wref[b * 8:b * 8 + 8].reshape(2 * SEGS, 2 * BLK))
            return 0

        lax.fori_loop(0, 2, part_of, 0)
        out_copy(b, REFS).start()

    far_start(1)
    for n in range(12):
        for side in range(2):
            halo_copy(n, side).wait_send()
    for c in x_copies:
        c.wait_send()
    for side in range(2):
        inv_copy(side).wait_send()
    for k in range(1):
        ag_copy(0, 7, k).wait_send()
    for b in range(BINS):
        for side in range(2):
            for n in range(3):
                gram_copy(b, side, n).wait_send()
                far_copy(b, side, n).wait()
        for group in range(5):
            out_copy(b, group).wait()


def select_kernel(pairs_ref, g_hbm, pair_out, ref_out, pair_buf, ref_buf, pair_sem, ref_sem):
    base = lax.axis_index("fibre") * NBLK
    copies = []
    for a in range(NBLK):
        for p in range(NP):
            e = pairs_ref[a, p] - base + NBLK
            slot = jnp.where(e >= 10, e + 2, e)
            copies.append((
                pltpu.make_async_copy(g_hbm.at[slot, :, a], pair_buf.at[a, p], pair_sem.at[0, a, p]),
                pltpu.make_async_copy(pair_buf.at[a, p], pair_out.at[:, a, p], pair_sem.at[1, a, p])))
    for r in range(2):
        copies.append((
            pltpu.make_async_copy(g_hbm.at[10 + r], ref_buf.at[r], ref_sem.at[0, r]),
            pltpu.make_async_copy(ref_buf.at[r], ref_out.at[:, :, r], ref_sem.at[1, r])))
    for c, _ in copies:
        c.start()
    for c, d in copies:
        c.wait()
        d.start()
    for _, d in copies:
        d.wait()


def body(spectra, pairs, refs):
    bf = jnp.bfloat16
    smem = pl.BlockSpec(memory_space=pltpu.SMEM)
    hbm = pl.BlockSpec(memory_space=pl.ANY)
    dma = pltpu.SemaphoreType.DMA
    grams = pl.pallas_call(
        kernel,
        out_shape=jax.ShapeDtypeStruct((SLOTS, BINS, NBLK, 2, BLK, BLK), bf),
        in_specs=[smem, hbm],
        out_specs=hbm,
        scratch_shapes=[
            pltpu.VMEM((2, BINS, 2, SEGS, PAIR), bf),
            pltpu.VMEM((2, BINS, 2, SEGS, PAIR), bf),
            pltpu.VMEM((BINS, 2, CHAN, 2 * SEGS), bf),
            pltpu.VMEM((2, BINS, 2, SEGS, 2 * BLK), bf),
            pltpu.VMEM((NZ, 128, 2 * BLK), bf),
            pltpu.VMEM((2, 9, 128, 2 * BLK), bf),
            pltpu.VMEM((144, 2 * BLK), bf),
            pltpu.VMEM((3, 144, 2 * BLK), bf),
            pltpu.VMEM((NZ, 144, 2 * BLK), bf),
            pltpu.VMEM((BINS, 5, 2, NBLK, 2, BLK, BLK), bf),
            pltpu.VMEM((BINS, 2, 3, 2, BLK, BLK), bf),
            pltpu.VMEM((BINS, 2, 3, 2, BLK, BLK), bf),
            pltpu.VMEM((BINS, 8, CHAN), jnp.float32),
            pltpu.VMEM((2, 8, CHAN), jnp.float32),
            pltpu.VMEM((BINS, 8, CHAN), jnp.float32),
            pltpu.VMEM((2, BINS, 8, 2 * BLK), jnp.float32),
            pltpu.VMEM((2, 16, CHAN), bf),
            pltpu.VMEM((NZ, 128, 2 * BLK), bf),
            dma((BINS, 2)),
            dma((2,)), dma((2,)),
            dma((2, 12)), dma((2, 12)),
            dma((2, 8, 2)), dma((2, 8, 2)),
            dma((3,)), dma((3,)),
            dma((2, 8, 2)), dma((2, 8, 2)),
            dma((BINS, 2, 3)), dma((BINS, 2, 3)),
            dma((2,)), dma((2,)),
            dma((BINS, 5)),
            dma((BINS, 2, 3)),
        ],
        compiler_params=pltpu.CompilerParams(
            collective_id=0, has_side_effects=True, vmem_limit_bytes=60 * 1024 * 1024),
        cost_estimate=pl.CostEstimate(
            flops=5_400_000_000, bytes_accessed=8 * 1024 * 1024, transcendentals=1024),
        name="grams",
    )(refs, spectra)
    return pl.pallas_call(
        select_kernel,
        out_shape=(
            jax.ShapeDtypeStruct((BINS, NBLK, NP, 2, BLK, BLK), bf),
            jax.ShapeDtypeStruct((BINS, NBLK, 2, 2, BLK, BLK), bf),
        ),
        in_specs=[smem, hbm],
        out_specs=(hbm, hbm),
        scratch_shapes=[
            pltpu.VMEM((NBLK, NP, BINS, 2, BLK, BLK), bf),
            pltpu.VMEM((2, BINS, NBLK, 2, BLK, BLK), bf),
            dma((2, NBLK, NP)), dma((2, 2)),
        ],
        compiler_params=pltpu.CompilerParams(vmem_limit_bytes=60 * 1024 * 1024),
        cost_estimate=pl.CostEstimate(
            flops=0, bytes_accessed=6 * 1024 * 1024, transcendentals=0),
        name="select",
    )(pairs, grams)


def solution(mesh):
    return jax.shard_map(
        body,
        mesh=mesh,
        in_specs=(P("freq", None, None, "fibre"), P("fibre", None), P()),
        out_specs=(
            P("freq", "fibre", None, None, None, None),
            P("freq", "fibre", None, None, None, None),
        ),
        check_vma=False,
    )
```
